256 devices in a mesh: row: 8 (over z), col: 32 (over x, y, core).
Axes of the slice: x: 4, y: 4, z: 8, core: 2. Of those that a mesh axis runs over, the one named last changes fastest.
Arguments:
- image_embeds: bfloat16 [16384, 1280], P(('row', 'col')), as said below
- text_embeds: bfloat16 [16384, 1280], P(('row', 'col'))
- labels: int32 [16384], P('row'), may hold values from 0 to 16383, as said below
Outputs:
- image_grad: bfloat16 [16384, 1280], P(('row', 'col'))
- text_grad: bfloat16 [16384, 1280], P(('row', 'col'))
The draws below stay inside these ranges and needn't reach their ends.
Inputs may be any that keep to these rules, and one draw needn't show every extreme that they name: `image_embeds`: entries of both embedding arrays lie within -18 to 18. labels is a permutation: each text is the match of exactly one image.
All inputs are finite; a program needn't handle non-finite values.
Results may differ from the reference program's by a relative error of at most 0.0045.
Values may be sent and summed in bfloat16 or wider, within the bound.
No kernel may reach another device: no remote copies, remote signals or barrier semaphores. Data moves between devices by JAX's collectives and lax.ppermute only.
A program may use at most 64 MiB of HBM per device.

```python
import jax
import jax.numpy as jnp
from jax import lax

D = 1280
N = 16384
N_ROW = 8


def shared_rows(key):
    first, second = jax.random.split(jax.random.fold_in(key, 7), 2)
    amplitude = (1500.0 / D) ** 0.5
    signs = jnp.sign(jax.random.normal(first, (N, D), jnp.float32) + 0.001)
    sizes = jax.random.uniform(second, (N, D), jnp.float32, 0.7, 1.3)
    return amplitude * signs * sizes


def pair_layout(key):
    key = jax.random.fold_in(key, 5)
    first, second, third, fourth = jax.random.split(key, 4)
    labels = jax.random.permutation(first, N).astype(jnp.int32)
    image_group = jax.random.randint(second, (N,), 0, 8, dtype=jnp.int32)
    text_group = jnp.zeros((N,), jnp.int32).at[labels].set(image_group)
    signs = jnp.sign(jax.random.normal(third, (8, D), jnp.float32) + 0.001)
    sizes = jax.random.uniform(fourth, (8, D), jnp.float32, 0.7, 1.3)
    centres = signs * sizes
    return (labels, image_group, text_group, centres)


def draw_labels(key, part):
    labels, image_group, text_group, centres = pair_layout(key)
    return labels


def draw_image_embeds(key, part):
    common = shared_rows(key)
    labels, image_group, text_group, centres = pair_layout(key)
    key = jax.random.fold_in(key, 11)
    first = jax.random.fold_in(key, 0)
    third = jax.random.fold_in(key, 2)
    strength = jax.random.uniform(third, (N, 1), jnp.float32, 1.0, 2.5)
    picked = jnp.arange(N)[:, None] % 64 == 0
    noise = jnp.clip(jax.random.normal(first, (N, D), jnp.float32), -6.0, 6.0)
    clustered = 0.65 * centres[image_group] + 0.4 * noise
    values = jnp.where(picked, strength * common, clustered)
    return values.astype(jnp.bfloat16)


def draw_text_embeds(key, part):
    common = shared_rows(key)
    labels, image_group, text_group, centres = pair_layout(key)
    key = jax.random.fold_in(key, 12)
    first = jax.random.fold_in(key, 0)
    noise = jnp.clip(jax.random.normal(first, (N, D), jnp.float32), -6.0, 6.0)
    clustered = 0.65 * centres[text_group] + 0.4 * noise
    position = jnp.arange(N)[:, None] % 64
    values = jnp.where(position == 0, common, clustered)
    values = jnp.where(position == 1, 1.01 * jnp.roll(common, 1, axis=0) + 0.1 * noise, values)
    return values.astype(jnp.bfloat16)


def setup_inputs(seed: int = 0) -> dict:
    splits = jax.random.split(jax.random.key(seed), 4)
    return {
        "image_embeds": draw_image_embeds(jax.random.fold_in(splits[3], 71), 0),
        "text_embeds": draw_text_embeds(jax.random.fold_in(splits[3], 71), 0),
        "labels": draw_labels(jax.random.fold_in(splits[3], 71), 0),
    }


score_scale = 0.1


def reference(image_embeds, text_embeds, labels):
    rows = N // N_ROW
    image_blocks = image_embeds.reshape(N_ROW, rows, D)
    label_blocks = labels.reshape(N_ROW, rows)
    columns = jnp.arange(N, dtype=jnp.int32)

    def scores_of(block):
        return score_scale * jnp.dot(block, text_embeds.T, preferred_element_type=jnp.float32)

    def first_pass(carry, item):
        col_max, col_sum = carry
        block = item
        scores = scores_of(block)
        top = jnp.max(scores, axis=1)
        row_lse = top + jnp.log(jnp.sum(jnp.exp(scores - top[:, None]), axis=1))
        new_max = jnp.maximum(col_max, jnp.max(scores, axis=0))
        col_sum = col_sum * jnp.exp(col_max - new_max) + jnp.sum(jnp.exp(scores - new_max[None, :]), axis=0)
        return (new_max, col_sum), row_lse

    start = (jnp.full((N,), -jnp.inf, jnp.float32), jnp.zeros((N,), jnp.float32))
    (col_max, col_sum), row_lse = lax.scan(first_pass, start, image_blocks)
    col_lse = col_max + jnp.log(col_sum)

    def second_pass(carry, item):
        block, block_labels, block_lse = item
        scores = scores_of(block)
        match = (block_labels[:, None] == columns[None, :]).astype(jnp.float32)
        dscores = (jnp.exp(scores - block_lse[:, None]) + jnp.exp(scores - col_lse[None, :]) - 2.0 * match).astype(jnp.bfloat16)
        image_part = (score_scale * jnp.dot(dscores, text_embeds, preferred_element_type=jnp.float32)).astype(jnp.bfloat16)
        carry = carry + jnp.dot(dscores.T, block, preferred_element_type=jnp.float32)
        return carry, image_part

    text_total, image_parts = lax.scan(second_pass, jnp.zeros((N, D), jnp.float32), (image_blocks, label_blocks, row_lse))
    image_grad = image_parts.reshape(N, D)
    text_grad = (score_scale * text_total).astype(jnp.bfloat16)
    return image_grad, text_grad
```

```python
import functools

import jax
import jax.numpy as jnp
from jax import lax
from jax.experimental import pallas as pl
from jax.experimental.pallas import tpu as pltpu
from jax.sharding import Mesh, PartitionSpec as P

score_scale = 0.1
lanes = 128
row_block = 256
vmem_bytes = 32 * 1024 * 1024
every = ("z", "x", "y", "core")
swap = [(0, 1), (1, 0)]


def statistics_groups():
    def device(z, x, y, core):
        return ((z * 4 + x) * 4 + y) * 2 + core

    columns = [
        [device(z, x + odd, y, 0) for odd in range(2) for z in range(8)] for x in (0, 2) for y in range(4)
    ]
    rows = [[device(z, x, y, 1) for x in range(4) for y in range(4)] for z in range(8)]
    return columns + rows


def scores_kernel(core, images, texts, scores, kept, sent, col_top, col_sum, rows_out):
    step = pl.program_id(0)
    s = score_scale * lax.dot_general(
        images[...], texts[...], (((1,), (1,)), ((), ())), preferred_element_type=jnp.float32
    )
    scores[...] = s
    top = jnp.max(s, axis=1, keepdims=True)
    row = top + jnp.log(jnp.sum(jnp.exp(s - top), axis=1, keepdims=True))
    row = jnp.broadcast_to(row, (s.shape[0], lanes)).T
    per_step = s.shape[0] // lanes
    for i in range(per_step):
        rows_out[pl.ds(step * per_step + i, 1), :] = row[:1, i * lanes : (i + 1) * lanes]

    @pl.when(step == 0)
    def _():
        col_top[...] = jnp.full(col_top.shape, -jnp.inf, jnp.float32)
        col_sum[...] = jnp.zeros(col_sum.shape, jnp.float32)

    old = col_top[...]
    new = jnp.maximum(old, jnp.max(s, axis=0, keepdims=True))
    total = col_sum[...] * jnp.exp(old - new) + jnp.sum(jnp.exp(s - new), axis=0, keepdims=True)
    col_top[...] = new
    col_sum[...] = total

    @pl.when(step == pl.num_programs(0) - 1)
    def _():
        col = new + jnp.log(total)
        first = core[0] == 0
        for i in range(kept.shape[0]):
            col_here = col[:, i * lanes : (i + 1) * lanes]
            row_here = rows_out[i : i + 1, :]
            kept[i : i + 1, :] = jnp.where(first, col_here, row_here)
            sent[i : i + 1, :] = jnp.where(first, row_here, col_here)


def local_scores(core, images, texts):
    rows, width = images.shape
    cols = texts.shape[0]
    steps = rows // row_block
    tile = (rows // lanes, lanes)
    return pl.pallas_call(
        scores_kernel,
        grid_spec=pltpu.PrefetchScalarGridSpec(
            num_scalar_prefetch=1,
            grid=(steps,),
            in_specs=[
                pl.BlockSpec((row_block, width), lambda i, c: (i, 0)),
                pl.BlockSpec((cols, width), lambda i, c: (0, 0)),
            ],
            out_specs=[
                pl.BlockSpec((row_block, cols), lambda i, c: (i, 0)),
                pl.BlockSpec(tile, lambda i, c: (0, 0)),
                pl.BlockSpec(tile, lambda i, c: (0, 0)),
            ],
            scratch_shapes=[
                pltpu.VMEM((1, cols), jnp.float32),
                pltpu.VMEM((1, cols), jnp.float32),
                pltpu.VMEM(tile, jnp.float32),
            ],
        ),
        out_shape=[
            jax.ShapeDtypeStruct((rows, cols), jnp.float32),
            jax.ShapeDtypeStruct(tile, jnp.float32),
            jax.ShapeDtypeStruct(tile, jnp.float32),
        ],
        compiler_params=pltpu.CompilerParams(vmem_limit_bytes=vmem_bytes),
        cost_estimate=pl.CostEstimate(
            flops=2 * rows * cols * width, bytes_accessed=10_000_000, transcendentals=2 * rows * cols
        ),
        name="scores",
    )(core, images, texts)


def merge_kernel(place, parts, kept, sent):
    def total(pieces):
        top = pieces[0]
        for piece in pieces[1:]:
            top = jnp.maximum(top, piece)
        sums = jnp.exp(pieces[0] - top)
        for piece in pieces[1:]:
            sums = sums + jnp.exp(piece - top)
        return top + jnp.log(sums)

    @pl.when(place[0] == 0)
    def _():
        first = place[1] * 8
        col = total([parts[first + z, core] for z in range(8) for core in range(2)])
        kept[...] = col
        sent[...] = col

    @pl.when(place[0] == 1)
    def _():
        sent[...] = total([parts[i, 0] for i in range(16)])
        kept[...] = total([parts[i, 1] for i in range(16)])


def merge(place, parts):
    tile = parts.shape[2:]
    return pl.pallas_call(
        merge_kernel,
        grid_spec=pltpu.PrefetchScalarGridSpec(
            num_scalar_prefetch=1,
            grid=(1,),
            in_specs=[pl.BlockSpec(parts.shape, lambda i, p: (0, 0, 0, 0))],
            out_specs=[pl.BlockSpec(tile, lambda i, p: (0, 0))] * 2,
        ),
        out_shape=[jax.ShapeDtypeStruct(tile, jnp.float32)] * 2,
        compiler_params=pltpu.CompilerParams(vmem_limit_bytes=vmem_bytes),
        name="merge",
    )(place, parts)


def dscores_kernel(core, scores, kept, received, targets, images, dscores, own, other, total):
    step = pl.program_id(0)
    rows, cols = scores.shape
    first = core[0] == 0
    per_step = rows // lanes
    col_lse = jnp.where(first, kept[...], received[...])
    here = pl.ds(step * per_step, per_step)
    row_here = jnp.where(first, received[here, :], kept[here, :])
    row_lse = jnp.concatenate(
        [jnp.broadcast_to(row_here[i : i + 1], (lanes, lanes)).T for i in range(per_step)], axis=0
    )
    target = targets[...]
    lane = lax.broadcasted_iota(jnp.int32, (rows, lanes), 1)
    for chunk in range(cols // lanes):
        part = slice(chunk * lanes, (chunk + 1) * lanes)
        s = scores[:, part]
        match = jnp.where(target == lane + chunk * lanes, 2.0, 0.0)
        dscores[:, part] = (
            jnp.exp(s - row_lse) + jnp.exp(s - col_lse[chunk : chunk + 1]) - match
        ).astype(jnp.bfloat16)

    @pl.when(step == 0)
    def _():
        total[...] = jnp.zeros(total.shape, jnp.float32)

    total[...] += lax.dot_general(
        dscores[...], images[...], (((0,), (0,)), ((), ())), preferred_element_type=jnp.float32
    )

    @pl.when(step == pl.num_programs(0) - 1)
    def _():
        piece = own.shape[0] // 8
        for z in range(8):
            rows_here = slice(z * piece, (z + 1) * piece)
            mine = pl.multiple_of((2 * z + core[0]) * piece, piece)
            theirs = pl.multiple_of((2 * z + 1 - core[0]) * piece, piece)
            own[rows_here] = total[pl.ds(mine, piece), :]
            other[rows_here] = total[pl.ds(theirs, piece), :].astype(jnp.bfloat16)


def local_dscores(core, scores, kept, received, targets, images):
    rows, cols = scores.shape
    width = images.shape[1]
    steps = rows // row_block
    return pl.pallas_call(
        dscores_kernel,
        grid_spec=pltpu.PrefetchScalarGridSpec(
            num_scalar_prefetch=1,
            grid=(steps,),
            in_specs=[
                pl.BlockSpec((row_block, cols), lambda i, c: (i, 0)),
                pl.BlockSpec(kept.shape, lambda i, c: (0, 0)),
                pl.BlockSpec(kept.shape, lambda i, c: (0, 0)),
                pl.BlockSpec((row_block, lanes), lambda i, c: (i, 0)),
                pl.BlockSpec((row_block, width), lambda i, c: (i, 0)),
            ],
            out_specs=[
                pl.BlockSpec((row_block, cols), lambda i, c: (i, 0)),
                pl.BlockSpec((cols // 2, width), lambda i, c: (0, 0)),
                pl.BlockSpec((cols // 2, width), lambda i, c: (0, 0)),
            ],
            scratch_shapes=[pltpu.VMEM((cols, width), jnp.float32)],
        ),
        out_shape=[
            jax.ShapeDtypeStruct((rows, cols), jnp.bfloat16),
            jax.ShapeDtypeStruct((cols // 2, width), jnp.float32),
            jax.ShapeDtypeStruct((cols // 2, width), jnp.bfloat16),
        ],
        compiler_params=pltpu.CompilerParams(vmem_limit_bytes=vmem_bytes),
        cost_estimate=pl.CostEstimate(
            flops=2 * rows * cols * width, bytes_accessed=12_000_000, transcendentals=2 * rows * cols
        ),
        name="dscores",
    )(core, scores, kept, received, targets, images)


def product_kernel(left, right, out):
    out[...] = jnp.dot(left[...], right[...], preferred_element_type=jnp.float32).astype(out.dtype)


def product(left, right):
    rows, depth = left.shape
    width = right.shape[1]
    return pl.pallas_call(
        product_kernel,
        grid=(rows // row_block,),
        in_specs=[
            pl.BlockSpec((row_block, depth), lambda i: (i, 0)),
            pl.BlockSpec((depth, width), lambda i: (0, 0)),
        ],
        out_specs=pl.BlockSpec((row_block, width), lambda i: (i, 0)),
        out_shape=jax.ShapeDtypeStruct((rows, width), jnp.bfloat16),
        compiler_params=pltpu.CompilerParams(vmem_limit_bytes=vmem_bytes),
        cost_estimate=pl.CostEstimate(
            flops=2 * rows * depth * width, bytes_accessed=8_000_000, transcendentals=0
        ),
        name="image_product",
    )(left, right)


def shards(image_embeds, text_embeds, labels):
    block, width = image_embeds.shape
    x, y, core = lax.axis_index("x"), lax.axis_index("y"), lax.axis_index("core")
    texts = lax.all_gather(text_embeds, ("z", "core"), axis=0, tiled=True)
    images = lax.all_to_all(
        jnp.broadcast_to(image_embeds, (16, block, width)), ("x", "y"), 0, 0, tiled=True
    ).reshape(16 * block, width)

    mine = lax.dynamic_index_in_dim(labels.reshape(16, 2, block), core, 1, keepdims=False).reshape(-1)
    pair = 2 * block
    plane = 16 * pair
    here = mine % plane // pair == x * 4 + y
    target = jnp.where(here, mine // plane * pair + mine % pair, -1)
    targets = jnp.broadcast_to(target[:, None], (16 * block, lanes))

    scores, kept, sent = local_scores(core.reshape(1), images, texts)
    received = lax.ppermute(sent, "core", swap)
    parts = jnp.stack([jnp.where(core == 0, kept, received), jnp.where(core == 0, received, kept)])
    parts = jnp.broadcast_to(parts, (16, *parts.shape))
    parts = lax.all_to_all(
        parts.reshape(256, lanes), every, 0, 0, axis_index_groups=statistics_groups(), tiled=True
    ).reshape(parts.shape)
    kept, sent = merge(jnp.stack([core, x % 2]), parts)
    received = lax.ppermute(sent, "core", swap)
    dscores, own, other = local_dscores(core.reshape(1), scores, kept, received, targets, images)
    theirs = lax.ppermute(other, "core", swap)
    image_term = product(dscores, texts)
    both = own + theirs.astype(jnp.float32)
    image_term, both = lax.optimization_barrier((image_term, both))
    text_total = lax.psum_scatter(both, "z", scatter_dimension=0, tiled=True)
    image_terms = lax.all_to_all(
        image_term.reshape(16, block, width), ("x", "y"), 0, 0, tiled=True
    )
    image_total = jnp.sum(image_terms.astype(jnp.float32), axis=0)
    image_grad = (score_scale * image_total).astype(jnp.bfloat16)
    text_grad = (score_scale * text_total).astype(jnp.bfloat16)
    return (image_grad, text_grad)


def solution(mesh):
    grid = Mesh(mesh.devices.reshape(8, 4, 4, 2), every)
    split = P(every, None)
    return jax.shard_map(
        shards, mesh=grid, in_specs=(split, split, P("z")), out_specs=(split, split), check_vma=False
    )
```

```python
import jax
import jax.numpy as jnp
from jax import lax
from jax.experimental import pallas as pl
from jax.experimental.pallas import tpu as pltpu
from jax.sharding import Mesh, PartitionSpec as P

score_scale = 0.1
lanes = 128
sizes = {"z": 8, "x": 4, "y": 4, "core": 2}
every = tuple(sizes)
offsets = (0, -1, 1, 2)
vmem_bytes = 24 * 1024 * 1024
in_vmem = pl.BlockSpec(memory_space=pltpu.VMEM)
in_smem = pl.BlockSpec(memory_space=pltpu.SMEM)
in_hbm = pl.BlockSpec(memory_space=pltpu.MemorySpace.HBM)
f32 = jnp.float32
bf16 = jnp.bfloat16


def device(z, x, y, core):
    return ((z % 8 * 4 + x % 4) * 4 + y % 4) * 2 + core


def send(value, move):
    pairs = [
        (device(z, x, y, core), device(*move(z, x, y, core)))
        for z in range(8)
        for x in range(4)
        for y in range(4)
        for core in range(2)
    ]
    return lax.ppermute(value, every, pairs)


def send_first(value, k):
    return send(value, lambda z, x, y, core: (z, x, y + k, 0) if core == 0 else (z, x + k, y, 1))


def send_second(value, k):
    return send(value, lambda z, x, y, core: (z, x + k, y, 0) if core == 0 else (z, x, y + k, 1))


def send_z(value, k):
    return send(value, lambda z, x, y, core: (z + k, x, y, 0) if core == 0 else (z - k, x, y, 1))


def swap_cores(value):
    return send(value, lambda z, x, y, core: (z, x, y, 1 - core))


def statistics_groups():
    columns = [
        [device(z, x + odd, y, 0) for odd in range(2) for z in range(8)] for x in (0, 2) for y in range(4)
    ]
    rows = [[device(z, x, y, 1) for x in range(4) for y in range(4)] for z in range(8)]
    return columns + rows


def row_tile(place, i, j):
    first = (place[1] + offsets[j]) & 3
    second = (place[2] + offsets[i]) & 3
    return jnp.where(place[0] == 0, second * 4 + first, first * 4 + second)


def scores_kernel(place, *refs):
    groups, pieces = refs[:4], refs[4:10]
    scores_out, texts_out, kept, sent, scores, texts, rows_out, sems = refs[10:]
    core, z = place[0], place[3]
    own, other = pieces[0], pieces[1]
    half = own.shape[0]
    pair = 2 * half
    side = 2 * core - 1

    def put(value, step, whose):
        start = pl.multiple_of(((z + step) & 7) * pair + whose * half, half)
        texts[pl.ds(start, half), :] = value

    put(own[...], 0, core)
    put(other[...], 0, 1 - core)
    for near, far, steps, whose in (
        (pieces[2], pieces[3], side, core),
        (pieces[4], pieces[5], -side, 1 - core),
    ):
        for k, piece in ((1, near[:pair]), (2, near[pair:]), (3, far[:pair])):
            put(piece[:half], steps * k, whose)
            put(piece[half:], steps * k, 1 - whose)
        put(far[pair:], 4, whose)

    rows_here = groups[0].shape[0]
    copies = [pltpu.make_async_copy(texts, texts_out, sems.at[4])]
    copies[0].start()
    for i in range(4):
        here = pl.ds(i * rows_here, rows_here)
        s = score_scale * lax.dot_general(
            groups[i][...], texts[...], (((1,), (1,)), ((), ())), preferred_element_type=f32
        )
        scores[here, :] = s
        copies.append(pltpu.make_async_copy(scores.at[here], scores_out.at[here], sems.at[i]))
        copies[-1].start()
        top = jnp.max(s, axis=1, keepdims=True)
        row = top + jnp.log(jnp.sum(jnp.exp(s - top), axis=1, keepdims=True))
        row = jnp.broadcast_to(row, (rows_here, lanes)).T
        for j in range(4):
            tile = row[:8, j // 2 * lanes : (j // 2 + 1) * lanes]
            if j % 2:
                tile = pltpu.roll(tile, half, 1)
            rows_out[pl.ds(row_tile(place, i, j), 1), :] = tile[:1]
        new = jnp.max(s, axis=0, keepdims=True)
        if i:
            new = jnp.maximum(col_top, new)
        total = jnp.sum(jnp.exp(s - new), axis=0, keepdims=True)
        if i:
            total = total + col_sum * jnp.exp(col_top - new)
        col_top, col_sum = new, total

    col = col_top + jnp.log(col_sum)
    first = core == 0
    for i in range(kept.shape[0]):
        row_here = rows_out[i : i + 1, :]
        k = i % (col.shape[1] // lanes)
        col_here = col[:, k * lanes : (k + 1) * lanes]
        kept[i : i + 1, :] = jnp.where(first, col_here, row_here)
        sent[i : i + 1, :] = jnp.where(first, row_here, col_here)
    for copy in copies:
        copy.wait()


def local_scores(place, groups, pieces):
    width = groups[0].shape[1]
    rows = 4 * groups[0].shape[0]
    cols = 16 * pieces[0].shape[0]
    tile = (16, lanes)
    return pl.pallas_call(
        scores_kernel,
        in_specs=[in_smem] + [in_vmem] * 10,
        out_specs=[in_hbm, in_hbm, in_vmem, in_vmem],
        out_shape=[
            pltpu.MemorySpace.HBM((rows, cols), f32),
            pltpu.MemorySpace.HBM((cols, width), bf16),
            jax.ShapeDtypeStruct(tile, f32),
            jax.ShapeDtypeStruct(tile, f32),
        ],
        scratch_shapes=[
            pltpu.VMEM((rows, cols), f32),
            pltpu.VMEM((cols, width), bf16),
            pltpu.VMEM(tile, f32),
            pltpu.SemaphoreType.DMA((5,)),
        ],
        compiler_params=pltpu.CompilerParams(vmem_limit_bytes=vmem_bytes),
        cost_estimate=pl.CostEstimate(
            flops=2 * rows * cols * width, bytes_accessed=6_000_000, transcendentals=2 * rows * cols
        ),
        name="scores",
    )(place, *groups, *pieces)


def spread_kernel(place, kept, received, out):
    first = place[0] == 0
    low = jnp.where(first, kept[...], received[...])
    high = jnp.where(first, received[...], kept[...])
    for i in range(out.shape[0]):
        out[i, 0] = low
        out[i, 1] = high


def spread(place, kept, received):
    return pl.pallas_call(
        spread_kernel,
        in_specs=[in_smem] + [in_vmem] * 2,
        out_specs=in_vmem,
        out_shape=jax.ShapeDtypeStruct((16, 2, *kept.shape), f32),
        compiler_params=pltpu.CompilerParams(vmem_limit_bytes=vmem_bytes),
        name="spread",
    )(place, kept, received)


def merge_kernel(place, parts, kept, sent):
    def total(pieces):
        top = pieces[0]
        for piece in pieces[1:]:
            top = jnp.maximum(top, piece)
        sums = jnp.exp(pieces[0] - top)
        for piece in pieces[1:]:
            sums = sums + jnp.exp(piece - top)
        return top + jnp.log(sums)

    @pl.when(place[0] == 0)
    def _():
        first = place[4] * 8
        col = total([parts[first + z, core] for z in range(8) for core in range(2)])
        kept[...] = col
        sent[...] = col

    @pl.when(place[0] == 1)
    def _():
        sent[...] = total([parts[i, 0] for i in range(16)])
        kept[...] = total([parts[i, 1] for i in range(16)])


def merge(place, parts):
    tile = parts.shape[2:]
    return pl.pallas_call(
        merge_kernel,
        in_specs=[in_smem, in_vmem],
        out_specs=[in_vmem] * 2,
        out_shape=[jax.ShapeDtypeStruct(tile, f32)] * 2,
        compiler_params=pltpu.CompilerParams(vmem_limit_bytes=vmem_bytes),
        name="merge",
    )(place, parts)


def dscores_kernel(
    place, scores_in, kept, received, labels, g0, g1, g2, g3, dscores, mine, theirs, scores, total, targets, sems
):
    core, z = place[0], place[3]
    first = core == 0
    half = lanes // 2
    rows_here = g0.shape[0]
    cols = scores.shape[1]
    copies = []
    for i in range(4):
        here = pl.ds(i * rows_here, rows_here)
        copies.append(pltpu.make_async_copy(scores_in.at[here], scores.at[here], sems.at[i]))
        copies[-1].start()
    label = labels[...]
    spot = place[5]
    target = jnp.where((label >> 7) & 15 == spot, (label >> 11) * lanes + (label & 127), -1).astype(f32)
    target = jnp.where(first, target, pltpu.roll(target, half, 1))
    lane_row = lax.broadcasted_iota(jnp.int32, (8, lanes), 1)
    lane = lax.broadcasted_iota(jnp.int32, (lanes, lanes), 1).astype(f32)

    def column(read, i, j):
        low = jnp.broadcast_to(read(row_tile(place, i, j)), (8, lanes))
        high = pltpu.roll(jnp.broadcast_to(read(row_tile(place, i, j + 1)), (8, lanes)), half, 1)
        both = jnp.where(lane_row < half, low, high)
        return jnp.broadcast_to(both[:1], (lanes, lanes)).T

    def row_lse(k):
        return jnp.where(first, received[pl.ds(k, 1), :], kept[pl.ds(k, 1), :])

    targets[...] = target

    def target_of(k):
        return targets[pl.ds(k, 1), :]

    col_lse = jnp.where(first, kept[...], received[...])
    for i in range(4):
        copies[i].wait()
        for j in (0, 2):
            row = column(row_lse, i, j)
            wanted = column(target_of, i, j)
            here = slice(i * rows_here + j * half, i * rows_here + j * half + lanes)
            for chunk in range(cols // lanes):
                part = slice(chunk * lanes, (chunk + 1) * lanes)
                s = scores[here, part]
                match = jnp.where(wanted == lane + float(chunk * lanes), 2.0, 0.0)
                dscores[here, part] = (
                    jnp.exp(s - row) + jnp.exp(s - col_lse[chunk : chunk + 1]) - match
                ).astype(bf16)

    images = jnp.concatenate([g0[...], g1[...], g2[...], g3[...]], axis=0)
    total[...] = lax.dot_general(
        dscores[...], images, (((0,), (0,)), ((), ())), preferred_element_type=f32
    )
    side = 1 - 2 * core

    def take(step, offset, size):
        return total[pl.ds(pl.multiple_of(((z + step) & 7) * lanes + offset, half), size), :]

    for k in range(1, 4):
        here = slice((k - 1) * lanes, k * lanes)
        mine[here, :] = take(side * k, 0, lanes)
        theirs[here, :] = take(-side * k, 0, lanes).astype(bf16)
    for k, step in ((6, 4), (7, 0)):
        here = slice(k * half, (k + 1) * half)
        mine[here, :] = take(step, core * half, half)
        theirs[here, :] = take(step, (1 - core) * half, half).astype(bf16)


def local_dscores(place, scores, kept, received, labels, groups):
    rows, cols = scores.shape
    width = groups[0].shape[1]
    return pl.pallas_call(
        dscores_kernel,
        in_specs=[in_smem, in_hbm] + [in_vmem] * 7,
        out_specs=[in_vmem] * 3,
        out_shape=[
            pltpu.VMEM((rows, cols), bf16),
            pltpu.VMEM((cols // 2, width), f32),
            pltpu.VMEM((cols // 2, width), bf16),
        ],
        scratch_shapes=[
            pltpu.VMEM((rows, cols), f32),
            pltpu.VMEM((cols, width), f32),
            pltpu.VMEM(labels.shape, f32),
            pltpu.SemaphoreType.DMA((4,)),
        ],
        compiler_params=pltpu.CompilerParams(vmem_limit_bytes=vmem_bytes),
        cost_estimate=pl.CostEstimate(
            flops=2 * rows * cols * width, bytes_accessed=6_000_000, transcendentals=2 * rows * cols
        ),
        name="dscores",
    )(place, scores, kept, received, labels, *groups)


def product_kernel(dscores, texts, *outs):
    rows_here = outs[0].shape[0]
    for i in (3, 1, 2, 0):
        outs[i][...] = jnp.dot(
            dscores[i * rows_here : (i + 1) * rows_here, :], texts[...], preferred_element_type=f32
        ).astype(outs[i].dtype)


def product(dscores, texts):
    rows, depth = dscores.shape
    width = texts.shape[1]
    return pl.pallas_call(
        product_kernel,
        in_specs=[in_vmem] * 2,
        out_specs=[in_vmem] * 4,
        out_shape=[pltpu.VMEM((rows // 4, width), f32 if i == 0 else bf16) for i in range(4)],
        compiler_params=pltpu.CompilerParams(vmem_limit_bytes=vmem_bytes),
        cost_estimate=pl.CostEstimate(
            flops=2 * rows * depth * width, bytes_accessed=6_000_000, transcendentals=0
        ),
        name="image_product",
    )(dscores, texts)


def add_text_kernel(mine, received, near, far, own):
    start = 0
    for out in (near, far, own):
        here = slice(start, start + out.shape[0])
        out[...] = (mine[here, :] + received[here, :].astype(f32)).astype(out.dtype)
        start += out.shape[0]


def add_text(mine, received):
    rows, width = mine.shape
    shapes = [(rows // 2, f32), (rows // 8 * 3, bf16), (rows // 8, f32)]
    return pl.pallas_call(
        add_text_kernel,
        in_specs=[in_vmem] * 2,
        out_specs=[in_vmem] * 3,
        out_shape=[pltpu.VMEM((n, width), kind) for n, kind in shapes],
        compiler_params=pltpu.CompilerParams(vmem_limit_bytes=vmem_bytes),
        cost_estimate=pl.CostEstimate(flops=rows * width, bytes_accessed=6 * rows * width, transcendentals=0),
        name="text_add",
    )(mine, received)


def relay_text_kernel(place, near, received, one, two):
    pair, half = one.shape[0], one.shape[0] // 2
    one[...] = (near[:pair] + received[:pair].astype(f32)).astype(bf16)
    two[...] = near[pair:].astype(bf16)
    here = pl.multiple_of(place[0] * half, half)
    two[pl.ds(here, half), :] = (
        near[pl.ds(pair + here, half), :] + received[pair:].astype(f32)
    ).astype(bf16)


def relay_text(place, near, received):
    rows, width = near.shape
    return pl.pallas_call(
        relay_text_kernel,
        in_specs=[in_smem] + [in_vmem] * 2,
        out_specs=[in_vmem] * 2,
        out_shape=[pltpu.VMEM((rows // 2, width), bf16)] * 2,
        compiler_params=pltpu.CompilerParams(vmem_limit_bytes=vmem_bytes),
        cost_estimate=pl.CostEstimate(flops=rows * width, bytes_accessed=6 * rows * width, transcendentals=0),
        name="text_relay",
    )(place, near, received)


def split_text_kernel(place, one, two, own, here, there):
    half = own.shape[0]
    core = place[0]

    def total(which):
        rows = pl.ds(pl.multiple_of(which * half, half), half)
        return one[rows, :].astype(f32) + two[rows, :].astype(f32)

    here[...] = total(core) + own[...]
    there[...] = total(1 - core)


def split_text(place, one, two, own):
    return pl.pallas_call(
        split_text_kernel,
        in_specs=[in_smem] + [in_vmem] * 3,
        out_specs=[in_vmem] * 2,
        out_shape=[pltpu.VMEM(own.shape, f32)] * 2,
        compiler_params=pltpu.CompilerParams(vmem_limit_bytes=vmem_bytes),
        cost_estimate=pl.CostEstimate(flops=4 * own.size, bytes_accessed=20 * own.size, transcendentals=0),
        name="text_split",
    )(place, one, two, own)


def join_kernel(*refs):
    out = refs[-1]
    start = 0
    for ref in refs[:-1]:
        size = min(ref.shape[0], out.shape[0] - start)
        out[start : start + size, :] = ref[:size, :]
        start += size


def join(rows, *parts):
    width = parts[0].shape[1]
    return pl.pallas_call(
        join_kernel,
        in_specs=[in_vmem] * len(parts),
        out_specs=in_vmem,
        out_shape=pltpu.VMEM((rows, width), bf16),
        compiler_params=pltpu.CompilerParams(vmem_limit_bytes=vmem_bytes),
        cost_estimate=pl.CostEstimate(flops=0, bytes_accessed=4 * rows * width, transcendentals=0),
        name="join",
    )(*parts)


def add_image_kernel(p0, p1, p2, p3, *outs):
    size = outs[0].shape[0]
    for j in range(4):
        here = slice(j * size, (j + 1) * size)
        outs[j][...] = (
            p0[here, :] + p1[here, :].astype(f32) + p2[here, :].astype(f32) + p3[here, :].astype(f32)
        )


def add_image(parts):
    rows, width = parts[0].shape
    return pl.pallas_call(
        add_image_kernel,
        in_specs=[in_vmem] * 4,
        out_specs=[in_vmem] * 4,
        out_shape=[pltpu.VMEM((rows // 4, width), f32)] * 4,
        compiler_params=pltpu.CompilerParams(vmem_limit_bytes=vmem_bytes),
        cost_estimate=pl.CostEstimate(
            flops=4 * rows * width, bytes_accessed=14 * rows * width, transcendentals=0
        ),
        name="image_add",
    )(*parts)


def gather(image_embeds, text_embeds):
    block = image_embeds.shape[0]
    line = [send_first(image_embeds, -k) for k in offsets[1:]]
    other = swap_cores(text_embeds)
    pair = join(2 * block, text_embeds, other)
    near = [send_z(pair, 2), send_z(pair, 1)]
    line, near = lax.optimization_barrier((line, near))
    line = join(4 * block, image_embeds, *line)
    ahead = join(3 * block, near[1], near[0])
    groups = [line] + [send_second(line, -k) for k in offsets[1:]]
    far = send_z(ahead, 2)
    near = join(4 * block, near[1], near[0])
    pieces = [text_embeds, other, near, far, swap_cores(near), swap_cores(far)]
    return groups, pieces


def shards(image_embeds, text_embeds, labels):
    z, x, y, core = (lax.axis_index(name) for name in every)
    along = [core, jnp.where(core == 0, y, x), jnp.where(core == 0, x, y), z, x & 1, x * 4 + y]
    place = jnp.stack(along).astype(jnp.int32)
    image_embeds, text_embeds, labels, place = lax.optimization_barrier(
        (image_embeds, text_embeds, labels, place)
    )
    groups, pieces = gather(image_embeds, text_embeds)
    scores, texts, kept, sent = local_scores(place, groups, pieces)
    parts = spread(place, kept, swap_cores(sent))
    parts = lax.all_to_all(
        parts.reshape(-1, lanes), every, 0, 0, axis_index_groups=statistics_groups(), tiled=True
    ).reshape(parts.shape)
    kept, sent = merge(place, parts)
    received = swap_cores(sent)

    dscores, mine, theirs = local_dscores(
        place, scores, kept, received, labels.reshape(-1, lanes), groups
    )
    theirs = swap_cores(theirs)
    terms = product(dscores, texts)
    near, far, own = add_text(mine, theirs)
    far = send_z(far, 2)
    parts = [send_second(t, k) for t, k in zip(terms[1:], offsets[1:])]
    far, parts = lax.optimization_barrier((far, parts))
    one, two = relay_text(place, near, far)
    terms = add_image([terms[0]] + parts)
    two, one = send_z(two, 2), send_z(one, 1)
    image_parts = [terms[0]] + [send_first(t, k) for t, k in zip(terms[1:], offsets[1:])]
    here, there = split_text(place, one, two, own)
    text_grad = (score_scale * (here + swap_cores(there))).astype(bf16)
    image_total = image_parts[0] + image_parts[1] + image_parts[2] + image_parts[3]
    image_grad = (score_scale * image_total).astype(bf16)
    return (image_grad, text_grad)


def solution(mesh):
    grid = Mesh(mesh.devices.reshape(tuple(sizes.values())), every)
    split = P(every, None)
    return jax.shard_map(
        shards, mesh=grid, in_specs=(split, split, P("z")), out_specs=(split, split), check_vma=False
    )
```

```python
import functools

import jax
import jax.numpy as jnp
from jax import lax
from jax.experimental import pallas as pl
from jax.experimental.pallas import tpu as pltpu
from jax.sharding import Mesh, PartitionSpec as P

score_scale = 0.1
lanes = 128
sizes = {"z": 8, "x": 4, "y": 4, "core": 2}
every = tuple(sizes)
offsets = (0, -1, 1, 2)
steps = (-3, 3, 4, -1, -2, 1, 2, 0)
vmem_bytes = 24 * 1024 * 1024
in_vmem = pl.BlockSpec(memory_space=pltpu.VMEM)
in_smem = pl.BlockSpec(memory_space=pltpu.SMEM)
in_hbm = pl.BlockSpec(memory_space=pltpu.MemorySpace.HBM)
f32 = jnp.float32
bf16 = jnp.bfloat16


def device(z, x, y, core):
    return ((z % 8 * 4 + x % 4) * 4 + y % 4) * 2 + core


def send(value, move):
    pairs = [
        (device(z, x, y, core), device(*move(z, x, y, core)))
        for z in range(8)
        for x in range(4)
        for y in range(4)
        for core in range(2)
    ]
    return lax.ppermute(value, every, pairs)


def send_first(value, k):
    return send(value, lambda z, x, y, core: (z, x, y + k, 0) if core == 0 else (z, x + k, y, 1))


def send_second(value, k):
    return send(value, lambda z, x, y, core: (z, x + k, y, 0) if core == 0 else (z, x, y + k, 1))


def send_z(value, k):
    return send(value, lambda z, x, y, core: (z + k, x, y, 0) if core == 0 else (z - k, x, y, 1))


def swap_cores(value):
    return send(value, lambda z, x, y, core: (z, x, y, 1 - core))


def statistics_groups():
    columns = [
        [device(z, x + odd, y, 0) for odd in range(2) for z in range(8)] for x in (0, 2) for y in range(4)
    ]
    rows = [[device(z, x, y, 1) for x in range(4) for y in range(4)] for z in range(8)]
    return columns + rows


def row_tile(place, i, j):
    first = (place[1] + offsets[j]) & 3
    second = (place[2] + offsets[i]) & 3
    return jnp.where(place[0] == 0, second * 4 + first, first * 4 + second)


def chunk_place(place, chunk):
    core = place[0]
    z = (place[3] + (2 * core - 1) * steps[chunk]) & 7
    return z, (1 - core if steps[chunk] < 0 else core) == 1


def scores_kernel(place, *refs):
    groups, pieces = refs[:4], refs[4:10]
    scores_out, texts_out, kept, sent, scores, texts, rows_out, cols_out, sems = refs[10:]
    own, other, near, far, other_near, other_far = pieces
    half = own.shape[0]
    pair = 2 * half
    start = 0
    for piece in (
        other_far[:pair], far[:pair], far[pair:], other_far[pair:], other_near[...], near[...], own[...], other[...]
    ):
        texts[start : start + piece.shape[0], :] = piece
        start += piece.shape[0]

    rows_here = groups[0].shape[0]
    copies = [pltpu.make_async_copy(texts, texts_out, sems.at[4])]
    copies[0].start()
    for i in range(4):
        here = pl.ds(i * rows_here, rows_here)
        s = score_scale * lax.dot_general(
            groups[i][...], texts[...], (((1,), (1,)), ((), ())), preferred_element_type=f32
        )
        scores[here, :] = s
        copies.append(pltpu.make_async_copy(scores.at[here], scores_out.at[here], sems.at[i]))
        copies[-1].start()
        top = jnp.max(s, axis=1, keepdims=True)
        row = top + jnp.log(jnp.sum(jnp.exp(s - top), axis=1, keepdims=True))
        row = jnp.broadcast_to(row, (rows_here, lanes)).T
        for j in range(4):
            tile = row[:8, j // 2 * lanes : (j // 2 + 1) * lanes]
            if j % 2:
                tile = pltpu.roll(tile, half, 1)
            rows_out[pl.ds(row_tile(place, i, j), 1), :] = tile[:1]
        new = jnp.max(s, axis=0, keepdims=True)
        if i:
            new = jnp.maximum(col_top, new)
        total = jnp.sum(jnp.exp(s - new), axis=0, keepdims=True)
        if i:
            total = total + col_sum * jnp.exp(col_top - new)
        col_top, col_sum = new, total

    col = col_top + jnp.log(col_sum)
    cols_out[...] = jnp.zeros(cols_out.shape, f32)
    for chunk in range(len(steps)):
        z, turned = chunk_place(place, chunk)
        tile = jnp.broadcast_to(col[:, chunk * lanes : (chunk + 1) * lanes], (8, lanes))
        tile = jnp.where(turned, pltpu.roll(tile, half, 1), tile)
        cols_out[pl.ds(z, 1), :] = tile[:1]
    first = place[0] == 0
    kept[...] = jnp.where(first, cols_out[...], rows_out[...])
    sent[...] = jnp.where(first, rows_out[...], cols_out[...])
    for copy in copies:
        copy.wait()


def local_scores(place, groups, pieces):
    width = groups[0].shape[1]
    rows = 4 * groups[0].shape[0]
    cols = 16 * pieces[0].shape[0]
    tile = (16, lanes)
    return pl.pallas_call(
        scores_kernel,
        in_specs=[in_smem] + [in_vmem] * 10,
        out_specs=[in_hbm, in_hbm, in_vmem, in_vmem],
        out_shape=[
            pltpu.MemorySpace.HBM((rows, cols), f32),
            pltpu.MemorySpace.HBM((cols, width), bf16),
            jax.ShapeDtypeStruct(tile, f32),
            jax.ShapeDtypeStruct(tile, f32),
        ],
        scratch_shapes=[
            pltpu.VMEM((rows, cols), f32),
            pltpu.VMEM((cols, width), bf16),
            pltpu.VMEM(tile, f32),
            pltpu.VMEM(tile, f32),
            pltpu.SemaphoreType.DMA((5,)),
        ],
        compiler_params=pltpu.CompilerParams(vmem_limit_bytes=vmem_bytes),
        cost_estimate=pl.CostEstimate(
            flops=2 * rows * cols * width, bytes_accessed=6_000_000, transcendentals=2 * rows * cols
        ),
        name="scores",
    )(place, *groups, *pieces)


def spread_kernel(place, kept, received, out):
    first = place[0] == 0
    low = jnp.where(first, kept[...], received[...])
    high = jnp.where(first, received[...], kept[...])
    for i in range(out.shape[0]):
        out[i, 0] = low
        out[i, 1] = high


def spread(place, kept, received):
    return pl.pallas_call(
        spread_kernel,
        in_specs=[in_smem] + [in_vmem] * 2,
        out_specs=in_vmem,
        out_shape=jax.ShapeDtypeStruct((16, 2, *kept.shape), f32),
        compiler_params=pltpu.CompilerParams(vmem_limit_bytes=vmem_bytes),
        name="spread",
    )(place, kept, received)


def merge_kernel(place, parts, kept, sent):
    def total(pieces):
        top = pieces[0]
        for piece in pieces[1:]:
            top = jnp.maximum(top, piece)
        sums = jnp.exp(pieces[0] - top)
        for piece in pieces[1:]:
            sums = sums + jnp.exp(piece - top)
        return top + jnp.log(sums)

    @pl.when(place[0] == 0)
    def _():
        first = place[4] * 8
        col = total([parts[first + z, core] for z in range(8) for core in range(2)])
        kept[...] = col
        sent[...] = col

    @pl.when(place[0] == 1)
    def _():
        sent[...] = total([parts[i, 0] for i in range(16)])
        kept[...] = total([parts[i, 1] for i in range(16)])


def merge(place, parts):
    tile = parts.shape[2:]
    return pl.pallas_call(
        merge_kernel,
        in_specs=[in_smem, in_vmem],
        out_specs=[in_vmem] * 2,
        out_shape=[jax.ShapeDtypeStruct(tile, f32)] * 2,
        compiler_params=pltpu.CompilerParams(vmem_limit_bytes=vmem_bytes),
        name="merge",
    )(place, parts)


def text_product(dscores, columns, images):
    return lax.dot_general(
        dscores[:, columns], images, (((0,), (0,)), ((), ())), preferred_element_type=f32
    )


def dscores_kernel(
    place, scores_in, kept, received, labels, g0, g1, g2, g3, dscores, mine, theirs, scores, targets, sems
):
    core, z, spot = place[0], place[3], place[5]
    first = core == 0
    half = lanes // 2
    rows_here = g0.shape[0]
    copies = []
    for i in range(4):
        here = pl.ds(i * rows_here, rows_here)
        copies.append(pltpu.make_async_copy(scores_in.at[here], scores.at[here], sems.at[i]))
        copies[-1].start()

    label = labels[...]
    step = ((2 * core - 1) * ((label >> 11) - z)) & 7
    chunk = jnp.zeros(label.shape, jnp.int32)
    for i in range(1, len(steps)):
        chunk = jnp.where(step == (steps[i] & 7), i, chunk)
    leading = jnp.where(step > 4, 1 - core, core)
    target = chunk * lanes + jnp.where((label >> 6) & 1 == leading, 0, half) + (label & (half - 1))
    target = jnp.where((label >> 7) & 15 == spot, target, -1).astype(f32)
    targets[...] = jnp.where(first, target, pltpu.roll(target, half, 1))

    lane_row = lax.broadcasted_iota(jnp.int32, (8, lanes), 1)
    lane = lax.broadcasted_iota(jnp.int32, (lanes, lanes), 1).astype(f32)

    def column(read, i, j):
        low = jnp.broadcast_to(read(row_tile(place, i, j)), (8, lanes))
        high = pltpu.roll(jnp.broadcast_to(read(row_tile(place, i, j + 1)), (8, lanes)), half, 1)
        both = jnp.where(lane_row < half, low, high)
        return jnp.broadcast_to(both[:1], (lanes, lanes)).T

    def row_lse(k):
        return jnp.where(first, received[pl.ds(k, 1), :], kept[pl.ds(k, 1), :])

    def target_of(k):
        return targets[pl.ds(k, 1), :]

    col_lse = []
    for i in range(len(steps)):
        k, turned = chunk_place(place, i)
        tile = jnp.where(first, kept[pl.ds(k, 1), :], received[pl.ds(k, 1), :])
        tile = jnp.broadcast_to(tile, (8, lanes))
        col_lse.append(jnp.where(turned, pltpu.roll(tile, half, 1), tile)[:1])
    for i in range(4):
        copies[i].wait()
        for j in (0, 2):
            row = column(row_lse, i, j)
            wanted = column(target_of, i, j)
            here = slice(i * rows_here + j * half, i * rows_here + j * half + lanes)
            for chunk in range(len(steps)):
                part = slice(chunk * lanes, (chunk + 1) * lanes)
                s = scores[here, part]
                match = jnp.where(wanted == lane + float(chunk * lanes), 2.0, 0.0)
                dscores[here, part] = (jnp.exp(s - row) + jnp.exp(s - col_lse[chunk]) - match).astype(bf16)

    images = jnp.concatenate([g0[...], g1[...], g2[...], g3[...]], axis=0)
    far = text_product(dscores, slice(0, 3 * lanes), images)
    mine[:lanes, :] = far[:lanes]
    mine[lanes:, :] = far[2 * lanes : 2 * lanes + half]
    theirs[:lanes, :] = far[lanes : 2 * lanes].astype(bf16)
    theirs[lanes:, :] = far[2 * lanes + half :].astype(bf16)


def local_dscores(place, scores, kept, received, labels, groups):
    rows, cols = scores.shape
    width = groups[0].shape[1]
    part = cols // 16 * 3
    scores = pltpu.with_memory_space_constraint(scores, pltpu.MemorySpace.HBM)
    return pl.pallas_call(
        dscores_kernel,
        in_specs=[in_smem, in_hbm] + [in_vmem] * 7,
        out_specs=[in_vmem] * 3,
        out_shape=[
            pltpu.VMEM((rows, cols), bf16),
            pltpu.VMEM((part, width), f32),
            pltpu.VMEM((part, width), bf16),
        ],
        scratch_shapes=[
            pltpu.VMEM((rows, cols), f32),
            pltpu.VMEM(labels.shape, f32),
            pltpu.SemaphoreType.DMA((4,)),
        ],
        compiler_params=pltpu.CompilerParams(vmem_limit_bytes=vmem_bytes),
        cost_estimate=pl.CostEstimate(
            flops=rows * cols * width, bytes_accessed=6_000_000, transcendentals=2 * rows * cols
        ),
        name="dscores",
    )(place, scores, kept, received, labels, *groups)


def near_kernel(dscores, g0, g1, g2, g3, after, mine, t1, t2, t3):
    half = lanes // 2
    images = jnp.concatenate([g0[...], g1[...], g2[...], g3[...]], axis=0)
    near = text_product(dscores, slice(3 * lanes, dscores.shape[1]), images)
    mine[: 2 * lanes, :] = near[: 2 * lanes]
    mine[2 * lanes :, :] = near[4 * lanes : 4 * lanes + half]
    t1[...] = near[2 * lanes : 3 * lanes].astype(bf16)
    t2[...] = near[3 * lanes : 4 * lanes].astype(bf16)
    t3[...] = near[4 * lanes + half :].astype(bf16)


def near_texts(dscores, groups, after):
    rows, cols = dscores.shape
    width = groups[0].shape[1]
    part = cols // 16 * 5
    return pl.pallas_call(
        near_kernel,
        in_specs=[in_vmem] * 6,
        out_specs=[in_vmem] * 4,
        out_shape=[pltpu.VMEM((part, width), f32)]
        + [pltpu.VMEM((n, width), bf16) for n in (lanes, lanes, lanes // 2)],
        compiler_params=pltpu.CompilerParams(vmem_limit_bytes=vmem_bytes),
        cost_estimate=pl.CostEstimate(
            flops=2 * rows * cols * width, bytes_accessed=6_000_000, transcendentals=0
        ),
        name="near_texts",
    )(dscores, *groups, after)


def product_kernel(dscores, texts, *outs):
    rows_here = outs[0].shape[0]
    for i in (3, 1, 2, 0):
        outs[i][...] = jnp.dot(
            dscores[i * rows_here : (i + 1) * rows_here, :], texts[...], preferred_element_type=f32
        ).astype(outs[i].dtype)


def product(dscores, texts):
    rows, depth = dscores.shape
    width = texts.shape[1]
    return pl.pallas_call(
        product_kernel,
        in_specs=[in_vmem] * 2,
        out_specs=[in_vmem] * 4,
        out_shape=[pltpu.VMEM((rows // 4, width), f32 if i == 0 else bf16) for i in range(4)],
        compiler_params=pltpu.CompilerParams(vmem_limit_bytes=vmem_bytes),
        cost_estimate=pl.CostEstimate(
            flops=2 * rows * depth * width, bytes_accessed=6_000_000, transcendentals=0
        ),
        name="image_product",
    )(dscores, texts)


def add_far_kernel(mine, received, out):
    out[...] = (mine[...] + received[...].astype(f32)).astype(bf16)


def add_far(mine, received):
    return pl.pallas_call(
        add_far_kernel,
        in_specs=[in_vmem] * 2,
        out_specs=in_vmem,
        out_shape=pltpu.VMEM(mine.shape, bf16),
        compiler_params=pltpu.CompilerParams(vmem_limit_bytes=vmem_bytes),
        cost_estimate=pl.CostEstimate(flops=mine.size, bytes_accessed=8 * mine.size, transcendentals=0),
        name="text_far",
    )(mine, received)


def relay_text_kernel(mine, t1, t2, t3, far, one, two, own):
    pair, half = one.shape[0], own.shape[0]

    one[...] = (mine[:pair, :] + t1[...].astype(f32) + far[:pair, :].astype(f32)).astype(bf16)
    second = mine[pair : 2 * pair, :] + t2[...].astype(f32)
    two[:half, :] = second[:half].astype(bf16)
    two[half:, :] = (second[half:] + far[pair:, :].astype(f32)).astype(bf16)
    own[...] = mine[2 * pair :, :] + t3[...].astype(f32)


def relay_text(mine, received, far):
    rows, width = mine.shape
    pair = rows // 5 * 2
    return pl.pallas_call(
        relay_text_kernel,
        in_specs=[in_vmem] * 5,
        out_specs=[in_vmem] * 3,
        out_shape=[
            pltpu.VMEM((pair, width), bf16),
            pltpu.VMEM((pair, width), bf16),
            pltpu.VMEM((pair // 2, width), f32),
        ],
        compiler_params=pltpu.CompilerParams(vmem_limit_bytes=vmem_bytes),
        cost_estimate=pl.CostEstimate(flops=10_000_000_000, bytes_accessed=10 * mine.size, transcendentals=0),
        name="text_relay",
    )(mine, *received, far)


def split_text_kernel(one, two, own, here, there):
    half = own.shape[0]
    here[...] = one[half:, :].astype(f32) + two[half:, :].astype(f32) + own[...]
    there[...] = one[:half, :].astype(f32) + two[:half, :].astype(f32)


def split_text(one, two, own):
    return pl.pallas_call(
        split_text_kernel,
        in_specs=[in_vmem] * 3,
        out_specs=[in_vmem] * 2,
        out_shape=[pltpu.VMEM(own.shape, f32)] * 2,
        compiler_params=pltpu.CompilerParams(vmem_limit_bytes=vmem_bytes),
        cost_estimate=pl.CostEstimate(flops=4 * own.size, bytes_accessed=20 * own.size, transcendentals=0),
        name="text_split",
    )(one, two, own)


def join_kernel(count, *refs):
    out = refs[-1]
    start = 0
    for ref in refs[:count]:
        size = min(ref.shape[0], out.shape[0] - start)
        out[start : start + size, :] = ref[:size, :]
        start += size


def join(rows, *parts, after=()):
    width = parts[0].shape[1]
    return pl.pallas_call(
        functools.partial(join_kernel, len(parts)),
        in_specs=[in_vmem] * (len(parts) + len(after)),
        out_specs=in_vmem,
        out_shape=pltpu.VMEM((rows, width), bf16),
        compiler_params=pltpu.CompilerParams(vmem_limit_bytes=vmem_bytes),
        cost_estimate=pl.CostEstimate(flops=0, bytes_accessed=4 * rows * width, transcendentals=0),
        name="join",
    )(*parts, *after)


def add_image_kernel(p0, p1, p2, p3, *outs):
    size = outs[0].shape[0]
    for j in range(4):
        here = slice(j * size, (j + 1) * size)
        total = p0[here, :] + p1[here, :].astype(f32) + p2[here, :].astype(f32) + p3[here, :].astype(f32)
        outs[j][...] = total.astype(outs[j].dtype)


def add_image(parts):
    rows, width = parts[0].shape
    return pl.pallas_call(
        add_image_kernel,
        in_specs=[in_vmem] * 4,
        out_specs=[in_vmem] * 4,
        out_shape=[pltpu.VMEM((rows // 4, width), bf16 if j else f32) for j in range(4)],
        compiler_params=pltpu.CompilerParams(vmem_limit_bytes=vmem_bytes),
        cost_estimate=pl.CostEstimate(
            flops=4 * rows * width, bytes_accessed=14 * rows * width, transcendentals=0
        ),
        name="image_add",
    )(*parts)


def load_kernel(a, b, a_out, b_out, sems):
    copies = [pltpu.make_async_copy(a, a_out, sems.at[0]), pltpu.make_async_copy(b, b_out, sems.at[1])]
    for copy in copies:
        copy.start()
    for copy in copies:
        copy.wait()


def load(a, b):
    return pl.pallas_call(
        load_kernel,
        in_specs=[in_hbm] * 2,
        out_specs=[in_vmem] * 2,
        out_shape=[pltpu.VMEM(a.shape, a.dtype), pltpu.VMEM(b.shape, b.dtype)],
        scratch_shapes=[pltpu.SemaphoreType.DMA((2,))],
        compiler_params=pltpu.CompilerParams(vmem_limit_bytes=vmem_bytes),
        cost_estimate=pl.CostEstimate(flops=0, bytes_accessed=4 * a.size, transcendentals=0),
        name="load",
    )(
        pltpu.with_memory_space_constraint(a, pltpu.MemorySpace.HBM),
        pltpu.with_memory_space_constraint(b, pltpu.MemorySpace.HBM),
    )


def gather(image_embeds, text_embeds):
    block = image_embeds.shape[0]
    line = [send_first(image_embeds, -k) for k in offsets[1:]]
    other = swap_cores(text_embeds)
    image_embeds, text_embeds = load(image_embeds, text_embeds)
    pair = join(2 * block, text_embeds, other)
    near = [send_z(pair, 2), send_z(pair, 1)]
    line = join(4 * block, image_embeds, *line)
    ahead = join(3 * block, near[1], near[0], after=(line,))
    groups = [line] + [send_second(line, -k) for k in offsets[1:]]
    far = send_z(ahead, 2)
    near = join(4 * block, near[1], near[0], after=(line,))
    pieces = [text_embeds, other, near, far, swap_cores(near), swap_cores(far)]
    return groups, pieces


def shards(image_embeds, text_embeds, labels):
    z, x, y, core = (lax.axis_index(name) for name in every)
    along = [core, jnp.where(core == 0, y, x), jnp.where(core == 0, x, y), z, x & 1, x * 4 + y]
    place = jnp.stack(along).astype(jnp.int32)
    image_embeds, text_embeds, labels, place = lax.optimization_barrier(
        (image_embeds, text_embeds, labels, place)
    )
    groups, pieces = gather(image_embeds, text_embeds)
    scores, texts, kept, sent = local_scores(place, groups, pieces)
    parts = spread(place, kept, swap_cores(sent))
    parts = lax.all_to_all(
        parts.reshape(-1, lanes), every, 0, 0, axis_index_groups=statistics_groups(), tiled=True
    ).reshape(parts.shape)
    kept, sent = merge(place, parts)
    received = swap_cores(sent)

    dscores, mine, theirs = local_dscores(
        place, scores, kept, received, labels.reshape(-1, lanes), groups
    )
    theirs = swap_cores(theirs)
    terms = product(dscores, texts)
    far = send_z(add_far(mine, theirs), 2)
    parts = [send_second(t, k) for t, k in zip(terms[1:], offsets[1:])]
    mine, *theirs = near_texts(dscores, groups, terms[0])
    one, two, own = relay_text(mine, [swap_cores(t) for t in theirs], far)
    terms = add_image([terms[0]] + parts)
    two, one = send_z(two, 2), send_z(one, 1)
    image_parts = [terms[0]] + [send_first(t, k) for t, k in zip(terms[1:], offsets[1:])]
    here, there = split_text(one, two, own)
    text_grad = (score_scale * (here + swap_cores(there))).astype(bf16)
    image_total = sum(part.astype(f32) for part in image_parts)
    image_grad = (score_scale * image_total).astype(bf16)
    return (image_grad, text_grad)


def solution(mesh):
    grid = Mesh(mesh.devices.reshape(tuple(sizes.values())), every)
    split = P(every, None)
    return jax.shard_map(
        shards, mesh=grid, in_specs=(split, split, P("z")), out_specs=(split, split), check_vma=False
    )
```

```python
import functools

import jax
import jax.numpy as jnp
from jax import lax
from jax.experimental import pallas as pl
from jax.experimental.pallas import tpu as pltpu
from jax.sharding import Mesh, PartitionSpec as P

score_scale = 0.1
lanes = 128
sizes = {"z": 8, "x": 4, "y": 4, "core": 2}
every = tuple(sizes)
offsets = (0, -1, 1, 2)
steps = (-3, 3, 4, -1, -2, 1, 2, 0)
vmem_bytes = 24 * 1024 * 1024
in_vmem = pl.BlockSpec(memory_space=pltpu.VMEM)
in_smem = pl.BlockSpec(memory_space=pltpu.SMEM)
in_hbm = pl.BlockSpec(memory_space=pltpu.MemorySpace.HBM)
f32 = jnp.float32
bf16 = jnp.bfloat16


def device(z, x, y, core):
    return ((z % 8 * 4 + x % 4) * 4 + y % 4) * 2 + core


def send(value, move):
    pairs = [
        (device(z, x, y, core), device(*move(z, x, y, core)))
        for z in range(8)
        for x in range(4)
        for y in range(4)
        for core in range(2)
    ]
    return lax.ppermute(value, every, pairs)


def send_first(value, k):
    return send(value, lambda z, x, y, core: (z, x, y + k, 0) if core == 0 else (z, x + k, y, 1))


def send_second(value, k):
    return send(value, lambda z, x, y, core: (z, x + k, y, 0) if core == 0 else (z, x, y + k, 1))


def send_z(value, k):
    return send(value, lambda z, x, y, core: (z + k, x, y, 0) if core == 0 else (z - k, x, y, 1))


def swap_cores(value):
    return send(value, lambda z, x, y, core: (z, x, y, 1 - core))


def statistics_groups():
    columns = [
        [device(z, x + odd, y, 0) for odd in range(2) for z in range(8)] for x in (0, 2) for y in range(4)
    ]
    rows = [[device(z, x, y, 1) for x in range(4) for y in range(4)] for z in range(8)]
    return columns + rows


def row_tile(place, i, j):
    first = (place[1] + offsets[j]) & 3
    second = (place[2] + offsets[i]) & 3
    return jnp.where(place[0] == 0, second * 4 + first, first * 4 + second)


def chunk_place(place, chunk):
    core = place[0]
    z = (place[3] + (2 * core - 1) * steps[chunk]) & 7
    return z, (1 - core if steps[chunk] < 0 else core) == 1


def scores_kernel(place, *refs):
    groups, pieces = refs[:4], refs[4:10]
    scores_out, texts_out, kept, sent, scores, texts, rows_out, cols_out, sems = refs[10:]
    own, other, near, far, other_near, other_far = pieces
    half = own.shape[0]
    pair = 2 * half
    start = 0
    for piece in (
        other_far[:pair], far[:pair], far[pair:], other_far[pair:], other_near[...], near[...], own[...], other[...]
    ):
        texts[start : start + piece.shape[0], :] = piece
        start += piece.shape[0]

    rows_here = groups[0].shape[0]
    copies = [pltpu.make_async_copy(texts, texts_out, sems.at[4])]
    copies[0].start()
    for i in range(4):
        here = pl.ds(i * rows_here, rows_here)
        s = score_scale * lax.dot_general(
            groups[i][...], texts[...], (((1,), (1,)), ((), ())), preferred_element_type=f32
        )
        scores[here, :] = s
        copies.append(pltpu.make_async_copy(scores.at[here], scores_out.at[here], sems.at[i]))
        copies[-1].start()
        top = jnp.max(s, axis=1, keepdims=True)
        row = top + jnp.log(jnp.sum(jnp.exp(s - top), axis=1, keepdims=True))
        row = jnp.broadcast_to(row, (rows_here, lanes)).T
        for j in range(4):
            tile = row[:8, j // 2 * lanes : (j // 2 + 1) * lanes]
            if j % 2:
                tile = pltpu.roll(tile, half, 1)
            rows_out[pl.ds(row_tile(place, i, j), 1), :] = tile[:1]
        new = jnp.max(s, axis=0, keepdims=True)
        if i:
            new = jnp.maximum(col_top, new)
        total = jnp.sum(jnp.exp(s - new), axis=0, keepdims=True)
        if i:
            total = total + col_sum * jnp.exp(col_top - new)
        col_top, col_sum = new, total

    col = col_top + jnp.log(col_sum)
    for chunk in range(len(steps)):
        z, turned = chunk_place(place, chunk)
        tile = jnp.broadcast_to(col[:, chunk * lanes : (chunk + 1) * lanes], (8, lanes))
        tile = jnp.where(turned, pltpu.roll(tile, half, 1), tile)
        cols_out[pl.ds(z, 1), :] = tile[:1]
    first = place[0] == 0
    lane = lax.broadcasted_iota(jnp.int32, (8, lanes), 1)
    for i in range(kept.shape[0]):
        low = jnp.broadcast_to(rows_out[2 * i : 2 * i + 1, :], (8, lanes))
        high = jnp.broadcast_to(rows_out[2 * i + 1 : 2 * i + 2, :], (8, lanes))
        row = jnp.where(lane < half, low, pltpu.roll(high, half, 1))[:1]
        col = cols_out[i : i + 1, :]
        kept[i : i + 1, :] = jnp.where(first, col, row)
        sent[i : i + 1, :] = jnp.where(first, row, col)
    for copy in copies:
        copy.wait()


def local_scores(place, groups, pieces):
    width = groups[0].shape[1]
    rows = 4 * groups[0].shape[0]
    cols = 16 * pieces[0].shape[0]
    tile = (8, lanes)
    return pl.pallas_call(
        scores_kernel,
        in_specs=[in_smem] + [in_vmem] * 10,
        out_specs=[in_hbm, in_hbm, in_vmem, in_vmem],
        out_shape=[
            pltpu.MemorySpace.HBM((rows, cols), f32),
            pltpu.MemorySpace.HBM((cols, width), bf16),
            jax.ShapeDtypeStruct(tile, f32),
            jax.ShapeDtypeStruct(tile, f32),
        ],
        scratch_shapes=[
            pltpu.VMEM((rows, cols), f32),
            pltpu.VMEM((cols, width), bf16),
            pltpu.VMEM((16, lanes), f32),
            pltpu.VMEM(tile, f32),
            pltpu.SemaphoreType.DMA((5,)),
        ],
        compiler_params=pltpu.CompilerParams(vmem_limit_bytes=vmem_bytes),
        cost_estimate=pl.CostEstimate(
            flops=2 * rows * cols * width, bytes_accessed=6_000_000, transcendentals=2 * rows * cols
        ),
        name="scores",
    )(place, *groups, *pieces)


def spread_kernel(place, kept, received, out):
    first = place[0] == 0
    low = jnp.where(first, kept[...], received[...])
    high = jnp.where(first, received[...], kept[...])
    for i in range(out.shape[0]):
        out[i, 0] = low
        out[i, 1] = high


def spread(place, kept, received):
    return pl.pallas_call(
        spread_kernel,
        in_specs=[in_smem] + [in_vmem] * 2,
        out_specs=in_vmem,
        out_shape=jax.ShapeDtypeStruct((16, 2, *kept.shape), f32),
        compiler_params=pltpu.CompilerParams(vmem_limit_bytes=vmem_bytes),
        name="spread",
    )(place, kept, received)


def merge_kernel(place, parts, kept, sent):
    def total(pieces):
        top = pieces[0]
        for piece in pieces[1:]:
            top = jnp.maximum(top, piece)
        sums = jnp.exp(pieces[0] - top)
        for piece in pieces[1:]:
            sums = sums + jnp.exp(piece - top)
        return top + jnp.log(sums)

    @pl.when(place[0] == 0)
    def _():
        first = place[4] * 8
        col = total([parts[first + z, core] for z in range(8) for core in range(2)])
        kept[...] = col
        sent[...] = col

    @pl.when(place[0] == 1)
    def _():
        sent[...] = total([parts[i, 0] for i in range(16)])
        kept[...] = total([parts[i, 1] for i in range(16)])


def merge(place, parts):
    tile = parts.shape[2:]
    return pl.pallas_call(
        merge_kernel,
        in_specs=[in_smem, in_vmem],
        out_specs=[in_vmem] * 2,
        out_shape=[jax.ShapeDtypeStruct(tile, f32)] * 2,
        compiler_params=pltpu.CompilerParams(vmem_limit_bytes=vmem_bytes),
        name="merge",
    )(place, parts)


def text_product(dscores, columns, images):
    return lax.dot_general(
        dscores[:, columns], images, (((0,), (0,)), ((), ())), preferred_element_type=f32
    )


def dscores_kernel(
    place, scores_in, kept, received, labels, g0, g1, g2, g3, dscores, mine, theirs, scores, targets, rows, sems
):
    core, z, spot = place[0], place[3], place[5]
    first = core == 0
    half = lanes // 2
    rows_here = g0.shape[0]
    copies = []
    for i in range(4):
        here = pl.ds(i * rows_here, rows_here)
        copies.append(pltpu.make_async_copy(scores_in.at[here], scores.at[here], sems.at[i]))
        copies[-1].start()

    label = labels[...]
    step = ((2 * core - 1) * ((label >> 11) - z)) & 7
    chunk = jnp.zeros(label.shape, jnp.int32)
    for i in range(1, len(steps)):
        chunk = jnp.where(step == (steps[i] & 7), i, chunk)
    leading = jnp.where(step > 4, 1 - core, core)
    target = chunk * lanes + jnp.where((label >> 6) & 1 == leading, 0, half) + (label & (half - 1))
    target = jnp.where((label >> 7) & 15 == spot, target, -1).astype(f32)
    targets[...] = jnp.where(first, target, pltpu.roll(target, half, 1))

    lane_row = lax.broadcasted_iota(jnp.int32, (8, lanes), 1)
    lane = lax.broadcasted_iota(jnp.int32, (lanes, lanes), 1).astype(f32)

    def column(read, i, j):
        low = jnp.broadcast_to(read(row_tile(place, i, j)), (8, lanes))
        high = pltpu.roll(jnp.broadcast_to(read(row_tile(place, i, j + 1)), (8, lanes)), half, 1)
        both = jnp.where(lane_row < half, low, high)
        return jnp.broadcast_to(both[:1], (lanes, lanes)).T

    for i in range(kept.shape[0]):
        tile = jnp.where(first, received[i : i + 1, :], kept[i : i + 1, :])
        rows[2 * i : 2 * i + 1, :] = tile
        rows[2 * i + 1 : 2 * i + 2, :] = pltpu.roll(jnp.broadcast_to(tile, (8, lanes)), half, 1)[:1]

    def row_lse(k):
        return rows[pl.ds(k, 1), :]

    def target_of(k):
        return targets[pl.ds(k, 1), :]

    col_lse = []
    for i in range(len(steps)):
        k, turned = chunk_place(place, i)
        tile = jnp.where(first, kept[pl.ds(k, 1), :], received[pl.ds(k, 1), :])
        tile = jnp.broadcast_to(tile, (8, lanes))
        col_lse.append(jnp.where(turned, pltpu.roll(tile, half, 1), tile)[:1])
    for i in range(4):
        copies[i].wait()
        for j in (0, 2):
            row = column(row_lse, i, j)
            wanted = column(target_of, i, j)
            here = slice(i * rows_here + j * half, i * rows_here + j * half + lanes)
            for chunk in range(len(steps)):
                part = slice(chunk * lanes, (chunk + 1) * lanes)
                s = scores[here, part]
                match = jnp.where(wanted == lane + float(chunk * lanes), 2.0, 0.0)
                dscores[here, part] = (jnp.exp(s - row) + jnp.exp(s - col_lse[chunk]) - match).astype(bf16)

    images = jnp.concatenate([g0[...], g1[...], g2[...], g3[...]], axis=0)
    far = text_product(dscores, slice(0, 3 * lanes), images)
    mine[:lanes, :] = far[:lanes]
    mine[lanes:, :] = far[2 * lanes : 2 * lanes + half]
    theirs[:lanes, :] = far[lanes : 2 * lanes].astype(bf16)
    theirs[lanes:, :] = far[2 * lanes + half :].astype(bf16)


def local_dscores(place, scores, kept, received, labels, groups):
    rows, cols = scores.shape
    width = groups[0].shape[1]
    part = cols // 16 * 3
    scores = pltpu.with_memory_space_constraint(scores, pltpu.MemorySpace.HBM)
    return pl.pallas_call(
        dscores_kernel,
        in_specs=[in_smem, in_hbm] + [in_vmem] * 7,
        out_specs=[in_vmem] * 3,
        out_shape=[
            pltpu.VMEM((rows, cols), bf16),
            pltpu.VMEM((part, width), f32),
            pltpu.VMEM((part, width), bf16),
        ],
        scratch_shapes=[
            pltpu.VMEM((rows, cols), f32),
            pltpu.VMEM(labels.shape, f32),
            pltpu.VMEM(labels.shape, f32),
            pltpu.SemaphoreType.DMA((4,)),
        ],
        compiler_params=pltpu.CompilerParams(vmem_limit_bytes=vmem_bytes),
        cost_estimate=pl.CostEstimate(
            flops=rows * cols * width, bytes_accessed=6_000_000, transcendentals=2 * rows * cols
        ),
        name="dscores",
    )(place, scores, kept, received, labels, *groups)


def near_kernel(dscores, g0, g1, g2, g3, after, mine, t1, t2, t3):
    half = lanes // 2
    images = jnp.concatenate([g0[...], g1[...], g2[...], g3[...]], axis=0)
    near = text_product(dscores, slice(3 * lanes, dscores.shape[1]), images)
    mine[: 2 * lanes, :] = near[: 2 * lanes]
    mine[2 * lanes :, :] = near[4 * lanes : 4 * lanes + half]
    t1[...] = near[2 * lanes : 3 * lanes].astype(bf16)
    t2[...] = near[3 * lanes : 4 * lanes].astype(bf16)
    t3[...] = near[4 * lanes + half :].astype(bf16)


def near_texts(dscores, groups, after):
    rows, cols = dscores.shape
    width = groups[0].shape[1]
    part = cols // 16 * 5
    return pl.pallas_call(
        near_kernel,
        in_specs=[in_vmem] * 6,
        out_specs=[in_vmem] * 4,
        out_shape=[pltpu.VMEM((part, width), f32)]
        + [pltpu.VMEM((n, width), bf16) for n in (lanes, lanes, lanes // 2)],
        compiler_params=pltpu.CompilerParams(vmem_limit_bytes=vmem_bytes),
        cost_estimate=pl.CostEstimate(
            flops=2 * rows * cols * width, bytes_accessed=6_000_000, transcendentals=0
        ),
        name="near_texts",
    )(dscores, *groups, after)


def product_kernel(dscores, texts, *outs):
    rows_here = outs[0].shape[0]
    for i in (3, 1, 2, 0):
        outs[i][...] = jnp.dot(
            dscores[i * rows_here : (i + 1) * rows_here, :], texts[...], preferred_element_type=f32
        ).astype(outs[i].dtype)


def product(dscores, texts):
    rows, depth = dscores.shape
    width = texts.shape[1]
    return pl.pallas_call(
        product_kernel,
        in_specs=[in_vmem] * 2,
        out_specs=[in_vmem] * 4,
        out_shape=[pltpu.VMEM((rows // 4, width), f32 if i == 0 else bf16) for i in range(4)],
        compiler_params=pltpu.CompilerParams(vmem_limit_bytes=vmem_bytes),
        cost_estimate=pl.CostEstimate(
            flops=2 * rows * depth * width, bytes_accessed=6_000_000, transcendentals=0
        ),
        name="image_product",
    )(dscores, texts)


def add_far_kernel(mine, received, out):
    out[...] = (mine[...] + received[...].astype(f32)).astype(bf16)


def add_far(mine, received):
    return pl.pallas_call(
        add_far_kernel,
        in_specs=[in_vmem] * 2,
        out_specs=in_vmem,
        out_shape=pltpu.VMEM(mine.shape, bf16),
        compiler_params=pltpu.CompilerParams(vmem_limit_bytes=vmem_bytes),
        cost_estimate=pl.CostEstimate(flops=mine.size, bytes_accessed=8 * mine.size, transcendentals=0),
        name="text_far",
    )(mine, received)


def relay_text_kernel(mine, t1, t2, t3, far, one, two, own):
    pair, half = one.shape[0], own.shape[0]

    one[...] = (mine[:pair, :] + t1[...].astype(f32) + far[:pair, :].astype(f32)).astype(bf16)
    second = mine[pair : 2 * pair, :] + t2[...].astype(f32)
    two[:half, :] = second[:half].astype(bf16)
    two[half:, :] = (second[half:] + far[pair:, :].astype(f32)).astype(bf16)
    own[...] = mine[2 * pair :, :] + t3[...].astype(f32)


def relay_text(mine, received, far):
    rows, width = mine.shape
    pair = rows // 5 * 2
    return pl.pallas_call(
        relay_text_kernel,
        in_specs=[in_vmem] * 5,
        out_specs=[in_vmem] * 3,
        out_shape=[
            pltpu.VMEM((pair, width), bf16),
            pltpu.VMEM((pair, width), bf16),
            pltpu.VMEM((pair // 2, width), f32),
        ],
        compiler_params=pltpu.CompilerParams(vmem_limit_bytes=vmem_bytes),
        cost_estimate=pl.CostEstimate(flops=10_000_000_000, bytes_accessed=10 * mine.size, transcendentals=0),
        name="text_relay",
    )(mine, *received, far)


def split_text_kernel(one, two, own, here, there):
    half = own.shape[0]
    here[...] = one[half:, :].astype(f32) + two[half:, :].astype(f32) + own[...]
    there[...] = one[:half, :].astype(f32) + two[:half, :].astype(f32)


def split_text(one, two, own):
    return pl.pallas_call(
        split_text_kernel,
        in_specs=[in_vmem] * 3,
        out_specs=[in_vmem] * 2,
        out_shape=[pltpu.VMEM(own.shape, f32)] * 2,
        compiler_params=pltpu.CompilerParams(vmem_limit_bytes=vmem_bytes),
        cost_estimate=pl.CostEstimate(flops=4 * own.size, bytes_accessed=20 * own.size, transcendentals=0),
        name="text_split",
    )(one, two, own)


def join_kernel(count, *refs):
    out = refs[-1]
    start = 0
    for ref in refs[:count]:
        size = min(ref.shape[0], out.shape[0] - start)
        out[start : start + size, :] = ref[:size, :]
        start += size


def join(rows, *parts, after=()):
    width = parts[0].shape[1]
    return pl.pallas_call(
        functools.partial(join_kernel, len(parts)),
        in_specs=[in_vmem] * (len(parts) + len(after)),
        out_specs=in_vmem,
        out_shape=pltpu.VMEM((rows, width), bf16),
        compiler_params=pltpu.CompilerParams(vmem_limit_bytes=vmem_bytes),
        cost_estimate=pl.CostEstimate(flops=0, bytes_accessed=4 * rows * width, transcendentals=0),
        name="join",
    )(*parts, *after)


def add_image_kernel(p0, p1, p2, p3, *outs):
    size = outs[0].shape[0]
    for j in range(4):
        here = slice(j * size, (j + 1) * size)
        total = p0[here, :] + p1[here, :].astype(f32) + p2[here, :].astype(f32) + p3[here, :].astype(f32)
        outs[j][...] = total.astype(outs[j].dtype)


def add_image(parts):
    rows, width = parts[0].shape
    return pl.pallas_call(
        add_image_kernel,
        in_specs=[in_vmem] * 4,
        out_specs=[in_vmem] * 4,
        out_shape=[pltpu.VMEM((rows // 4, width), bf16 if j else f32) for j in range(4)],
        compiler_params=pltpu.CompilerParams(vmem_limit_bytes=vmem_bytes),
        cost_estimate=pl.CostEstimate(
            flops=4 * rows * width, bytes_accessed=14 * rows * width, transcendentals=0
        ),
        name="image_add",
    )(*parts)


def load_kernel(a, b, a_out, b_out, sems):
    copies = [pltpu.make_async_copy(a, a_out, sems.at[0]), pltpu.make_async_copy(b, b_out, sems.at[1])]
    for copy in copies:
        copy.start()
    for copy in copies:
        copy.wait()


def load(a, b):
    return pl.pallas_call(
        load_kernel,
        in_specs=[in_hbm] * 2,
        out_specs=[in_vmem] * 2,
        out_shape=[pltpu.VMEM(a.shape, a.dtype), pltpu.VMEM(b.shape, b.dtype)],
        scratch_shapes=[pltpu.SemaphoreType.DMA((2,))],
        compiler_params=pltpu.CompilerParams(vmem_limit_bytes=vmem_bytes),
        cost_estimate=pl.CostEstimate(flops=0, bytes_accessed=4 * a.size, transcendentals=0),
        name="load",
    )(
        pltpu.with_memory_space_constraint(a, pltpu.MemorySpace.HBM),
        pltpu.with_memory_space_constraint(b, pltpu.MemorySpace.HBM),
    )


def gather(image_embeds, text_embeds):
    block = image_embeds.shape[0]
    line = [send_first(image_embeds, -k) for k in offsets[1:]]
    other = swap_cores(text_embeds)
    image_embeds, text_embeds = load(image_embeds, text_embeds)
    pair = join(2 * block, text_embeds, other)
    near = [send_z(pair, 2), send_z(pair, 1)]
    line = join(4 * block, image_embeds, *line)
    ahead = join(3 * block, near[1], near[0], after=(line,))
    groups = [line] + [send_second(line, -k) for k in offsets[1:]]
    far = send_z(ahead, 2)
    near = join(4 * block, near[1], near[0], after=(line,))
    pieces = [text_embeds, other, near, far, swap_cores(near), swap_cores(far)]
    return groups, pieces


def shards(image_embeds, text_embeds, labels):
    z, x, y, core = (lax.axis_index(name) for name in every)
    along = [core, jnp.where(core == 0, y, x), jnp.where(core == 0, x, y), z, x & 1, x * 4 + y]
    place = jnp.stack(along).astype(jnp.int32)
    image_embeds, text_embeds, labels, place = lax.optimization_barrier(
        (image_embeds, text_embeds, labels, place)
    )
    groups, pieces = gather(image_embeds, text_embeds)
    scores, texts, kept, sent = local_scores(place, groups, pieces)
    parts = spread(place, kept, swap_cores(sent))
    parts = lax.all_to_all(
        parts.reshape(-1, lanes), every, 0, 0, axis_index_groups=statistics_groups(), tiled=True
    ).reshape(parts.shape)
    kept, sent = merge(place, parts)
    received = swap_cores(sent)

    dscores, mine, theirs = local_dscores(
        place, scores, kept, received, labels.reshape(-1, lanes), groups
    )
    theirs = swap_cores(theirs)
    terms = product(dscores, texts)
    far = send_z(add_far(mine, theirs), 2)
    parts = [send_second(t, k) for t, k in zip(terms[1:], offsets[1:])]
    mine, *theirs = near_texts(dscores, groups, terms[0])
    one, two, own = relay_text(mine, [swap_cores(t) for t in theirs], far)
    terms = add_image([terms[0]] + parts)
    two, one = send_z(two, 2), send_z(one, 1)
    image_parts = [terms[0]] + [send_first(t, k) for t, k in zip(terms[1:], offsets[1:])]
    here, there = split_text(one, two, own)
    text_grad = (score_scale * (here + swap_cores(there))).astype(bf16)
    image_total = sum(part.astype(f32) for part in image_parts)
    image_grad = (score_scale * image_total).astype(bf16)
    return (image_grad, text_grad)


def solution(mesh):
    grid = Mesh(mesh.devices.reshape(tuple(sizes.values())), every)
    split = P(every, None)
    return jax.shard_map(
        shards, mesh=grid, in_specs=(split, split, P("z")), out_specs=(split, split), check_vma=False
    )
```

```python
import functools

import jax
import jax.numpy as jnp
from jax import lax
from jax.experimental import pallas as pl
from jax.experimental.pallas import tpu as pltpu
from jax.sharding import Mesh, PartitionSpec as P

score_scale = 0.1
lanes = 128
sizes = {"z": 8, "x": 4, "y": 4, "core": 2}
every = tuple(sizes)
offsets = (0, -1, 1, 2)
steps = (-3, 3, 4, -1, -2, 1, 2, 0)
vmem_bytes = 24 * 1024 * 1024
in_vmem = pl.BlockSpec(memory_space=pltpu.VMEM)
in_smem = pl.BlockSpec(memory_space=pltpu.SMEM)
in_hbm = pl.BlockSpec(memory_space=pltpu.MemorySpace.HBM)
f32 = jnp.float32
bf16 = jnp.bfloat16


def device(z, x, y, core):
    return ((z % 8 * 4 + x % 4) * 4 + y % 4) * 2 + core


def send(value, move):
    pairs = [
        (device(z, x, y, core), device(*move(z, x, y, core)))
        for z in range(8)
        for x in range(4)
        for y in range(4)
        for core in range(2)
    ]
    return lax.ppermute(value, every, pairs)


def send_first(value, k):
    return send(value, lambda z, x, y, core: (z, x, y + k, 0) if core == 0 else (z, x + k, y, 1))


def send_second(value, k):
    return send(value, lambda z, x, y, core: (z, x + k, y, 0) if core == 0 else (z, x, y + k, 1))


def send_z(value, k):
    return send(value, lambda z, x, y, core: (z + k, x, y, 0) if core == 0 else (z - k, x, y, 1))


def swap_cores(value):
    return send(value, lambda z, x, y, core: (z, x, y, 1 - core))


def statistics_groups():
    columns = [
        [device(z, x + odd, y, 0) for odd in range(2) for z in range(8)] for x in (0, 2) for y in range(4)
    ]
    rows = [[device(z, x, y, 1) for x in range(4) for y in range(4)] for z in range(8)]
    return columns + rows


def row_tile(place, i, j):
    first = (place[1] + offsets[j]) & 3
    second = (place[2] + offsets[i]) & 3
    return jnp.where(place[0] == 0, second * 4 + first, first * 4 + second)


def chunk_place(place, chunk):
    core = place[0]
    z = (place[3] + (2 * core - 1) * steps[chunk]) & 7
    return z, (1 - core if steps[chunk] < 0 else core) == 1


def scores_kernel(place, *refs):
    groups, pieces = refs[:4], refs[4:10]
    scores_out, texts_out, kept, sent, scores, texts, rows_out, cols_out, sems = refs[10:]
    own, other, near, far, other_near, other_far = pieces
    half = own.shape[0]
    pair = 2 * half
    start = 0
    for piece in (
        other_far[:pair], far[:pair], far[pair:], other_far[pair:], other_near[...], near[...], own[...], other[...]
    ):
        texts[start : start + piece.shape[0], :] = piece
        start += piece.shape[0]

    rows_here = groups[0].shape[0]
    copies = [pltpu.make_async_copy(texts, texts_out, sems.at[4])]
    copies[0].start()
    for i in range(4):
        here = pl.ds(i * rows_here, rows_here)
        s = score_scale * lax.dot_general(
            groups[i][...], texts[...], (((1,), (1,)), ((), ())), preferred_element_type=f32
        )
        scores[here, :] = s
        copies.append(pltpu.make_async_copy(scores.at[here], scores_out.at[here], sems.at[i]))
        copies[-1].start()
        top = jnp.max(s, axis=1, keepdims=True)
        row = top + jnp.log(jnp.sum(jnp.exp(s - top), axis=1, keepdims=True))
        row = jnp.broadcast_to(row, (rows_here, lanes)).T
        for j in range(4):
            tile = row[:8, j // 2 * lanes : (j // 2 + 1) * lanes]
            if j % 2:
                tile = pltpu.roll(tile, half, 1)
            rows_out[pl.ds(row_tile(place, i, j), 1), :] = tile[:1]
        new = jnp.max(s, axis=0, keepdims=True)
        if i:
            new = jnp.maximum(col_top, new)
        total = jnp.sum(jnp.exp(s - new), axis=0, keepdims=True)
        if i:
            total = total + col_sum * jnp.exp(col_top - new)
        col_top, col_sum = new, total

    col = col_top + jnp.log(col_sum)
    for chunk in range(len(steps)):
        z, turned = chunk_place(place, chunk)
        tile = jnp.broadcast_to(col[:, chunk * lanes : (chunk + 1) * lanes], (8, lanes))
        tile = jnp.where(turned, pltpu.roll(tile, half, 1), tile)
        cols_out[pl.ds(z, 1), :] = tile[:1]
    first = place[0] == 0
    lane = lax.broadcasted_iota(jnp.int32, (8, lanes), 1)
    for i in range(kept.shape[0]):
        low = jnp.broadcast_to(rows_out[2 * i : 2 * i + 1, :], (8, lanes))
        high = jnp.broadcast_to(rows_out[2 * i + 1 : 2 * i + 2, :], (8, lanes))
        row = jnp.where(lane < half, low, pltpu.roll(high, half, 1))[:1]
        col = cols_out[i : i + 1, :]
        kept[i : i + 1, :] = jnp.where(first, col, row)
        sent[i : i + 1, :] = jnp.where(first, row, col)
    for copy in copies:
        copy.wait()


def local_scores(place, groups, pieces):
    width = groups[0].shape[1]
    rows = 4 * groups[0].shape[0]
    cols = 16 * pieces[0].shape[0]
    tile = (8, lanes)
    return pl.pallas_call(
        scores_kernel,
        in_specs=[in_smem] + [in_vmem] * 10,
        out_specs=[in_hbm, in_hbm, in_vmem, in_vmem],
        out_shape=[
            pltpu.MemorySpace.HBM((rows, cols), f32),
            pltpu.MemorySpace.HBM((cols, width), bf16),
            jax.ShapeDtypeStruct(tile, f32),
            jax.ShapeDtypeStruct(tile, f32),
        ],
        scratch_shapes=[
            pltpu.VMEM((rows, cols), f32),
            pltpu.VMEM((cols, width), bf16),
            pltpu.VMEM((16, lanes), f32),
            pltpu.VMEM(tile, f32),
            pltpu.SemaphoreType.DMA((5,)),
        ],
        compiler_params=pltpu.CompilerParams(vmem_limit_bytes=vmem_bytes),
        cost_estimate=pl.CostEstimate(
            flops=2 * rows * cols * width, bytes_accessed=6_000_000, transcendentals=2 * rows * cols
        ),
        name="scores",
    )(place, *groups, *pieces)


def spread_kernel(place, kept, received, out):
    first = place[0] == 0
    low = jnp.where(first, kept[...], received[...])
    high = jnp.where(first, received[...], kept[...])
    for i in range(out.shape[0]):
        out[i, 0] = low
        out[i, 1] = high


def spread(place, kept, received):
    return pl.pallas_call(
        spread_kernel,
        in_specs=[in_smem] + [in_vmem] * 2,
        out_specs=in_vmem,
        out_shape=jax.ShapeDtypeStruct((16, 2, *kept.shape), f32),
        compiler_params=pltpu.CompilerParams(vmem_limit_bytes=vmem_bytes),
        name="spread",
    )(place, kept, received)


def merge_kernel(place, parts, kept, sent):
    def total(pieces):
        top = pieces[0]
        for piece in pieces[1:]:
            top = jnp.maximum(top, piece)
        sums = jnp.exp(pieces[0] - top)
        for piece in pieces[1:]:
            sums = sums + jnp.exp(piece - top)
        return top + jnp.log(sums)

    @pl.when(place[0] == 0)
    def _():
        first = place[4] * 8
        col = total([parts[first + z, core] for z in range(8) for core in range(2)])
        kept[...] = col
        sent[...] = col

    @pl.when(place[0] == 1)
    def _():
        sent[...] = total([parts[i, 0] for i in range(16)])
        kept[...] = total([parts[i, 1] for i in range(16)])


def merge(place, parts):
    tile = parts.shape[2:]
    return pl.pallas_call(
        merge_kernel,
        in_specs=[in_smem, in_vmem],
        out_specs=[in_vmem] * 2,
        out_shape=[jax.ShapeDtypeStruct(tile, f32)] * 2,
        compiler_params=pltpu.CompilerParams(vmem_limit_bytes=vmem_bytes),
        name="merge",
    )(place, parts)


def text_product(dscores, columns, images):
    return lax.dot_general(
        dscores[:, columns], images, (((0,), (0,)), ((), ())), preferred_element_type=f32
    )


def dscores_kernel(
    place, scores_in, kept, received, labels, g0, g1, g2, g3, dscores, mine, theirs, scores, targets, rows, sems
):
    core, z, spot = place[0], place[3], place[5]
    first = core == 0
    half = lanes // 2
    rows_here = g0.shape[0]
    copies = []
    for i in range(4):
        here = pl.ds(i * rows_here, rows_here)
        copies.append(pltpu.make_async_copy(scores_in.at[here], scores.at[here], sems.at[i]))
        copies[-1].start()

    label = labels[...]
    step = ((2 * core - 1) * ((label >> 11) - z)) & 7
    chunk = jnp.zeros(label.shape, jnp.int32)
    for i in range(1, len(steps)):
        chunk = jnp.where(step == (steps[i] & 7), i, chunk)
    leading = jnp.where(step > 4, 1 - core, core)
    target = chunk * lanes + jnp.where((label >> 6) & 1 == leading, 0, half) + (label & (half - 1))
    target = jnp.where((label >> 7) & 15 == spot, target, -1).astype(f32)
    targets[...] = jnp.where(first, target, pltpu.roll(target, half, 1))

    lane_row = lax.broadcasted_iota(jnp.int32, (8, lanes), 1)
    lane = lax.broadcasted_iota(jnp.int32, (lanes, lanes), 1).astype(f32)

    def column(read, i, j):
        low = jnp.broadcast_to(read(row_tile(place, i, j)), (8, lanes))
        high = pltpu.roll(jnp.broadcast_to(read(row_tile(place, i, j + 1)), (8, lanes)), half, 1)
        both = jnp.where(lane_row < half, low, high)
        return jnp.broadcast_to(both[:1], (lanes, lanes)).T

    for i in range(kept.shape[0]):
        tile = jnp.where(first, received[i : i + 1, :], kept[i : i + 1, :])
        rows[2 * i : 2 * i + 1, :] = tile
        rows[2 * i + 1 : 2 * i + 2, :] = pltpu.roll(jnp.broadcast_to(tile, (8, lanes)), half, 1)[:1]

    def row_lse(k):
        return rows[pl.ds(k, 1), :]

    def target_of(k):
        return targets[pl.ds(k, 1), :]

    col_lse = []
    for i in range(len(steps)):
        k, turned = chunk_place(place, i)
        tile = jnp.where(first, kept[pl.ds(k, 1), :], received[pl.ds(k, 1), :])
        tile = jnp.broadcast_to(tile, (8, lanes))
        col_lse.append(jnp.where(turned, pltpu.roll(tile, half, 1), tile)[:1])
    for i in range(4):
        copies[i].wait()
        for j in (0, 2):
            row = column(row_lse, i, j)
            wanted = column(target_of, i, j)
            here = slice(i * rows_here + j * half, i * rows_here + j * half + lanes)
            for chunk in range(len(steps)):
                part = slice(chunk * lanes, (chunk + 1) * lanes)
                s = scores[here, part]
                match = jnp.where(wanted == lane + float(chunk * lanes), 2.0, 0.0)
                dscores[here, part] = (jnp.exp(s - row) + jnp.exp(s - col_lse[chunk]) - match).astype(bf16)

    images = jnp.concatenate([g0[...], g1[...], g2[...], g3[...]], axis=0)
    far = text_product(dscores, slice(0, 3 * lanes), images)
    mine[:lanes, :] = far[:lanes]
    mine[lanes:, :] = far[2 * lanes : 2 * lanes + half]
    theirs[:lanes, :] = far[lanes : 2 * lanes].astype(bf16)
    theirs[lanes:, :] = far[2 * lanes + half :].astype(bf16)


def local_dscores(place, scores, kept, received, labels, groups):
    rows, cols = scores.shape
    width = groups[0].shape[1]
    part = cols // 16 * 3
    scores = pltpu.with_memory_space_constraint(scores, pltpu.MemorySpace.HBM)
    return pl.pallas_call(
        dscores_kernel,
        in_specs=[in_smem, in_hbm] + [in_vmem] * 7,
        out_specs=[in_vmem] * 3,
        out_shape=[
            pltpu.VMEM((rows, cols), bf16),
            pltpu.VMEM((part, width), f32),
            pltpu.VMEM((part, width), bf16),
        ],
        scratch_shapes=[
            pltpu.VMEM((rows, cols), f32),
            pltpu.VMEM(labels.shape, f32),
            pltpu.VMEM(labels.shape, f32),
            pltpu.SemaphoreType.DMA((4,)),
        ],
        compiler_params=pltpu.CompilerParams(vmem_limit_bytes=vmem_bytes),
        cost_estimate=pl.CostEstimate(
            flops=rows * cols * width, bytes_accessed=6_000_000, transcendentals=2 * rows * cols
        ),
        name="dscores",
    )(place, scores, kept, received, labels, *groups)


def near_kernel(dscores, g0, g1, g2, g3, after, mine, t1, t2, t3):
    half = lanes // 2
    images = jnp.concatenate([g0[...], g1[...], g2[...], g3[...]], axis=0)
    near = text_product(dscores, slice(3 * lanes, dscores.shape[1]), images)
    mine[: 2 * lanes, :] = near[: 2 * lanes]
    mine[2 * lanes :, :] = near[4 * lanes : 4 * lanes + half]
    t1[...] = near[2 * lanes : 3 * lanes].astype(bf16)
    t2[...] = near[3 * lanes : 4 * lanes].astype(bf16)
    t3[...] = near[4 * lanes + half :].astype(bf16)


def near_texts(dscores, groups, after):
    rows, cols = dscores.shape
    width = groups[0].shape[1]
    part = cols // 16 * 5
    return pl.pallas_call(
        near_kernel,
        in_specs=[in_vmem] * 6,
        out_specs=[in_vmem] * 4,
        out_shape=[pltpu.VMEM((part, width), f32)]
        + [pltpu.VMEM((n, width), bf16) for n in (lanes, lanes, lanes // 2)],
        compiler_params=pltpu.CompilerParams(vmem_limit_bytes=vmem_bytes),
        cost_estimate=pl.CostEstimate(
            flops=2 * rows * cols * width, bytes_accessed=6_000_000, transcendentals=0
        ),
        name="near_texts",
    )(dscores, *groups, after)


def product_kernel(dscores, texts, *outs):
    rows_here = outs[0].shape[0]
    for i in (3, 1, 2, 0):
        outs[i][...] = jnp.dot(
            dscores[i * rows_here : (i + 1) * rows_here, :], texts[...], preferred_element_type=f32
        ).astype(outs[i].dtype)


def product(dscores, texts):
    rows, depth = dscores.shape
    width = texts.shape[1]
    return pl.pallas_call(
        product_kernel,
        in_specs=[in_vmem] * 2,
        out_specs=[in_vmem] * 4,
        out_shape=[pltpu.VMEM((rows // 4, width), f32 if i == 0 else bf16) for i in range(4)],
        compiler_params=pltpu.CompilerParams(vmem_limit_bytes=vmem_bytes),
        cost_estimate=pl.CostEstimate(
            flops=2 * rows * depth * width, bytes_accessed=6_000_000, transcendentals=0
        ),
        name="image_product",
    )(dscores, texts)


def add_far_kernel(mine, received, out):
    out[...] = (mine[...] + received[...].astype(f32)).astype(bf16)


def add_far(mine, received):
    return pl.pallas_call(
        add_far_kernel,
        in_specs=[in_vmem] * 2,
        out_specs=in_vmem,
        out_shape=pltpu.VMEM(mine.shape, bf16),
        compiler_params=pltpu.CompilerParams(vmem_limit_bytes=vmem_bytes),
        cost_estimate=pl.CostEstimate(flops=mine.size, bytes_accessed=8 * mine.size, transcendentals=0),
        name="text_far",
    )(mine, received)


def relay_text_kernel(mine, t1, t2, t3, far, one, two, own):
    pair, half = one.shape[0], own.shape[0]

    one[...] = (mine[:pair, :] + t1[...].astype(f32) + far[:pair, :].astype(f32)).astype(bf16)
    second = mine[pair : 2 * pair, :] + t2[...].astype(f32)
    two[:half, :] = second[:half].astype(bf16)
    two[half:, :] = (second[half:] + far[pair:, :].astype(f32)).astype(bf16)
    own[...] = mine[2 * pair :, :] + t3[...].astype(f32)


def relay_text(mine, received, far):
    rows, width = mine.shape
    pair = rows // 5 * 2
    return pl.pallas_call(
        relay_text_kernel,
        in_specs=[in_vmem] * 5,
        out_specs=[in_vmem] * 3,
        out_shape=[
            pltpu.VMEM((pair, width), bf16),
            pltpu.VMEM((pair, width), bf16),
            pltpu.VMEM((pair // 2, width), f32),
        ],
        compiler_params=pltpu.CompilerParams(vmem_limit_bytes=vmem_bytes),
        cost_estimate=pl.CostEstimate(flops=10_000_000_000, bytes_accessed=10 * mine.size, transcendentals=0),
        name="text_relay",
    )(mine, *received, far)


def split_text_kernel(one, two, own, here, there):
    half = own.shape[0]
    here[...] = one[half:, :].astype(f32) + two[half:, :].astype(f32) + own[...]
    there[...] = one[:half, :].astype(f32) + two[:half, :].astype(f32)


def split_text(one, two, own):
    return pl.pallas_call(
        split_text_kernel,
        in_specs=[in_vmem] * 3,
        out_specs=[in_vmem] * 2,
        out_shape=[pltpu.VMEM(own.shape, f32)] * 2,
        compiler_params=pltpu.CompilerParams(vmem_limit_bytes=vmem_bytes),
        cost_estimate=pl.CostEstimate(flops=4 * own.size, bytes_accessed=20 * own.size, transcendentals=0),
        name="text_split",
    )(one, two, own)


def join_kernel(count, *refs):
    out = refs[-1]
    start = 0
    for ref in refs[:count]:
        size = min(ref.shape[0], out.shape[0] - start)
        out[start : start + size, :] = ref[:size, :]
        start += size


def join(rows, *parts, after=()):
    width = parts[0].shape[1]
    return pl.pallas_call(
        functools.partial(join_kernel, len(parts)),
        in_specs=[in_vmem] * (len(parts) + len(after)),
        out_specs=in_vmem,
        out_shape=pltpu.VMEM((rows, width), bf16),
        compiler_params=pltpu.CompilerParams(vmem_limit_bytes=vmem_bytes),
        cost_estimate=pl.CostEstimate(flops=0, bytes_accessed=4 * rows * width, transcendentals=0),
        name="join",
    )(*parts, *after)


def add_image_kernel(p0, p1, p2, p3, *outs):
    size = outs[0].shape[0]
    for j in range(4):
        here = slice(j * size, (j + 1) * size)
        total = p0[here, :] + p1[here, :].astype(f32) + p2[here, :].astype(f32) + p3[here, :].astype(f32)
        outs[j][...] = total.astype(outs[j].dtype)


def add_image(parts):
    rows, width = parts[0].shape
    return pl.pallas_call(
        add_image_kernel,
        in_specs=[in_vmem] * 4,
        out_specs=[in_vmem] * 4,
        out_shape=[pltpu.VMEM((rows // 4, width), bf16 if j else f32) for j in range(4)],
        compiler_params=pltpu.CompilerParams(vmem_limit_bytes=vmem_bytes),
        cost_estimate=pl.CostEstimate(
            flops=4 * rows * width, bytes_accessed=14 * rows * width, transcendentals=0
        ),
        name="image_add",
    )(*parts)


def load_kernel(a, b, a_out, b_out, sems):
    copies = [pltpu.make_async_copy(a, a_out, sems.at[0]), pltpu.make_async_copy(b, b_out, sems.at[1])]
    for copy in copies:
        copy.start()
    for copy in copies:
        copy.wait()


def load(a, b):
    return pl.pallas_call(
        load_kernel,
        in_specs=[in_hbm] * 2,
        out_specs=[in_vmem] * 2,
        out_shape=[pltpu.VMEM(a.shape, a.dtype), pltpu.VMEM(b.shape, b.dtype)],
        scratch_shapes=[pltpu.SemaphoreType.DMA((2,))],
        compiler_params=pltpu.CompilerParams(vmem_limit_bytes=vmem_bytes),
        cost_estimate=pl.CostEstimate(flops=0, bytes_accessed=4 * a.size, transcendentals=0),
        name="load",
    )(
        pltpu.with_memory_space_constraint(a, pltpu.MemorySpace.HBM),
        pltpu.with_memory_space_constraint(b, pltpu.MemorySpace.HBM),
    )


def gather(image_embeds, text_embeds):
    block = image_embeds.shape[0]
    line = [send_first(image_embeds, -k) for k in offsets[1:]]
    other = swap_cores(text_embeds)
    image_embeds, text_embeds = load(image_embeds, text_embeds)
    pair = join(2 * block, text_embeds, other)
    near = [send_z(pair, 2), send_z(pair, 1)]
    line = join(4 * block, image_embeds, *line)
    ahead = join(3 * block, near[1], near[0], after=(line,))
    groups = [line] + [send_second(line, -k) for k in offsets[1:]]
    far = send_z(ahead, 2)
    near = join(4 * block, near[1], near[0], after=(line,))
    pieces = [text_embeds, other, near, far, swap_cores(near), swap_cores(far)]
    return groups, pieces


def shards(image_embeds, text_embeds, labels):
    z, x, y, core = (lax.axis_index(name) for name in every)
    along = [core, jnp.where(core == 0, y, x), jnp.where(core == 0, x, y), z, x & 1, x * 4 + y]
    place = jnp.stack(along).astype(jnp.int32)
    image_embeds, text_embeds, labels, place = lax.optimization_barrier(
        (image_embeds, text_embeds, labels, place)
    )
    groups, pieces = gather(image_embeds, text_embeds)
    scores, texts, kept, sent = local_scores(place, groups, pieces)
    parts = spread(place, kept, swap_cores(sent))
    parts = lax.all_to_all(
        parts.reshape(-1, lanes), every, 0, 0, axis_index_groups=statistics_groups(), tiled=True
    ).reshape(parts.shape)
    kept, sent = merge(place, parts)
    received = swap_cores(sent)

    dscores, mine, theirs = local_dscores(
        place, scores, kept, received, labels.reshape(-1, lanes), groups
    )
    theirs = swap_cores(theirs)
    terms = product(dscores, texts)
    far = send_z(add_far(mine, theirs), 2)
    last = send_second(terms[3], offsets[3])
    parts = [send_second(t, k) for t, k in zip(terms[1:3], offsets[1:3])] + [last]
    mine, *theirs = near_texts(dscores, groups, terms[0])
    one, two, own = relay_text(mine, [swap_cores(t) for t in theirs], far)
    terms = add_image([terms[0]] + parts)
    two, one = send_z(two, 2), send_z(one, 1)
    last = send_first(terms[3], offsets[3])
    image_parts = [terms[0]] + [send_first(t, k) for t, k in zip(terms[1:3], offsets[1:3])] + [last]
    here, there = split_text(one, two, own)
    text_grad = (score_scale * (here + swap_cores(there))).astype(bf16)
    image_total = sum(part.astype(f32) for part in image_parts)
    image_grad = (score_scale * image_total).astype(bf16)
    return (image_grad, text_grad)


def solution(mesh):
    grid = Mesh(mesh.devices.reshape(tuple(sizes.values())), every)
    split = P(every, None)
    return jax.shard_map(
        shards, mesh=grid, in_specs=(split, split, P("z")), out_specs=(split, split), check_vma=False
    )
```
